512 devices in a mesh: group: 8 (over z_lo, core), dp: 64 (over z_hi, y, x).
Axes of the slice: x: 4, y: 8, z: 8 (z_hi: 2, z_lo: 4; z = z_hi * 4 + z_lo), core: 2. Of those that a mesh axis runs over, the one named last changes fastest.
Arguments:
- tokens: bfloat16 [8192, 3072], P('dp', 'group'), may hold values from -6 to 6
- expert_ids: int32 [8192, 2], P('dp'), may hold values from 0 to 7, as said below
- gates: float32 [8192, 2], P('dp'), may hold values from 0.2 to 1
- gate_weight: bfloat16 [8192, 3072], P('dp', 'group'), may hold values from -0.109375 to 0.109375
- up_weight: bfloat16 [8192, 3072], P('dp', 'group'), may hold values from -0.109375 to 0.109375
- down_weight: bfloat16 [8192, 3072], P('dp', 'group'), may hold values from -0.0625 to 0.0625
- cotangent: bfloat16 [8192, 3072], P('dp', 'group'), may hold values from -6 to 6
Outputs:
- mixed: bfloat16 [8192, 3072], P('dp', 'group')
- token_grad: bfloat16 [8192, 3072], P('dp', 'group')
- gates_grad: float32 [8192, 2], P('dp')
- gate_weight_grad: float32 [8192, 3072], P('dp', 'group')
- up_weight_grad: float32 [8192, 3072], P('dp', 'group')
- down_weight_grad: float32 [8192, 3072], P('dp', 'group')
The draws below stay inside these ranges and needn't reach their ends.
Inputs may be any that keep to these rules, and one draw needn't show every extreme that they name: `expert_ids`: the 2 ids of a row differ. In each aligned block of 128 rows (the tokens of one index of dp) expert 0 is named by at least 16 and at most 20 rows, and by exactly 20 rows in some block.
All inputs are finite; a program needn't handle non-finite values.
Results may differ from the reference program's by a relative error of at most 0.022.
Values may be sent and summed in bfloat16 or wider, within the bound.
A program may use at most 64 MiB of HBM per device.

```python
import jax
import jax.numpy as jnp
from jax import lax

D = 3072
E = 8
TOPK = 2
P_SIZE = 8192
TOK_DEV = 128
TOKENS = 8192
CAP = 20
N_DP = 64


def draw_expert_ids(key, part):
    key = jax.random.fold_in(key, 11)
    blocks = TOKENS // TOK_DEV
    keys = jax.random.split(key, 6)
    counts = jax.random.randint(keys[0], (blocks,), CAP - CAP // 5, CAP + 1)
    star = jax.random.randint(keys[1], (), 0, blocks)
    counts = jnp.where(jnp.arange(blocks) == star, CAP, counts)
    scores = jax.random.randint(keys[2], (blocks, TOK_DEV), 0, 1 << 20) * TOK_DEV + jnp.arange(TOK_DEV)[None, :]
    order = jnp.argsort(scores, axis=1)
    ranks = jnp.argsort(order, axis=1)
    marked = ranks < counts[:, None]
    side = jax.random.randint(keys[3], (blocks, TOK_DEV), 0, 2)
    other = jax.random.randint(keys[4], (blocks, TOK_DEV), 1, E)
    offset = jax.random.randint(keys[5], (blocks, TOK_DEV), 1, E - 1)
    second = 1 + (other - 1 + offset) % (E - 1)
    first_id = jnp.where(marked, jnp.where(side == 0, 0, other), other)
    second_id = jnp.where(marked, jnp.where(side == 0, other, 0), second)
    return jnp.stack([first_id, second_id], axis=-1).reshape(TOKENS, TOPK).astype(jnp.int32)


def level_of(stream_key, dims, cuts, low, high):
    def one(axis_at, blocks):
        steps = jax.random.uniform(jax.random.fold_in(jax.random.fold_in(stream_key, 6), axis_at), (blocks,), jnp.float32, low / len(cuts), high / len(cuts))
        return jnp.repeat(jnp.exp(steps), dims[axis_at] // blocks).reshape((-1,) + (1,) * (len(dims) - axis_at - 1))

    gain = one(*cuts[0])
    for cut in cuts[1:]:
        gain = gain * one(*cut)
    return gain


def gaussian(stream_key, extent, scale, reach, cuts=(), kind=jnp.bfloat16):
    entries = jax.random.normal(stream_key, extent, jnp.float32) * scale
    if len(cuts) > 0:
        entries = level_of(stream_key, extent, cuts, -0.22, 0.18) * entries
    return jnp.clip(entries, min=-reach, max=reach).astype(kind)


def setup_inputs(seed: int = 0) -> dict:
    streams_of = jax.random.split(jax.random.key(seed), 8)
    return {
        "tokens": gaussian(streams_of[0], (TOKENS, D), 1.0, 6.0, ((0, 64), (1, 8))),
        "expert_ids": draw_expert_ids(jax.random.fold_in(streams_of[7], 71), 0),
        "gates": jnp.clip(0.2 + 0.8 * jax.random.uniform(streams_of[2], (TOKENS, TOPK), jnp.float32) ** level_of(streams_of[2], (TOKENS, TOPK), ((0, 64),), -0.2, 0.2), 0.2, 1.0),
        "gate_weight": gaussian(streams_of[3], (P_SIZE, D), D ** -0.5, 0.109375, ((0, 64), (1, 8))),
        "up_weight": gaussian(streams_of[4], (P_SIZE, D), D ** -0.5, 0.109375, ((0, 64), (1, 8))),
        "down_weight": gaussian(streams_of[5], (P_SIZE, D), P_SIZE ** -0.5, 0.0625, ((0, 64), (1, 8))),
        "cotangent": gaussian(streams_of[6], (TOKENS, D), 1.0, 6.0, ((0, 64), (1, 8))),
    }


def silu_parts(active):
    sigma = jax.nn.sigmoid(active)
    return active * sigma, sigma * (1.0 + active * (1.0 - sigma))


def inner_last(left, right):
    return lax.dot_general(left, right, (((1,), (1,)), ((), ())), preferred_element_type=jnp.float32)


def inner_first(left, right):
    return lax.dot_general(left, right, (((0,), (0,)), ((), ())), preferred_element_type=jnp.float32)


def reference(tokens, expert_ids, gates, gate_weight, up_weight, down_weight, cotangent):
    rows_all = N_DP * CAP
    blocks = TOKENS // TOK_DEV
    chosen = expert_ids == 0
    chosen_f = chosen.astype(jnp.float32)
    token_gate = jnp.sum(chosen_f * gates, axis=1)
    picked = jnp.max(chosen.astype(jnp.int32), axis=1).reshape(blocks, TOK_DEV)
    before = jnp.cumsum(picked, axis=1) - picked
    slot = jnp.arange(blocks, dtype=jnp.int32)[:, None] * CAP + before
    slot = jnp.where(picked > 0, slot, rows_all).reshape(-1).astype(jnp.int32)
    owners = jnp.arange(TOKENS, dtype=jnp.int32)
    table = jnp.full((rows_all,), TOKENS, dtype=jnp.int32).at[slot].set(owners, mode="drop")
    grad_rows = (token_gate[:, None] * cotangent.astype(jnp.float32)).astype(jnp.bfloat16)
    padded_tokens = jnp.concatenate([tokens, jnp.zeros((1, D), jnp.bfloat16)], axis=0)
    padded_grad = jnp.concatenate([grad_rows, jnp.zeros((1, D), jnp.bfloat16)], axis=0)
    inputs = padded_tokens[table]
    out_grad = padded_grad[table]
    gate_act = inner_last(inputs, gate_weight)
    up_act = inner_last(inputs, up_weight)
    silu_act, silu_slope = silu_parts(gate_act)
    hidden = (silu_act * up_act).astype(jnp.bfloat16)
    expert_out = jnp.dot(hidden, down_weight, preferred_element_type=jnp.float32).astype(jnp.bfloat16)
    hidden_grad = inner_last(out_grad, down_weight)
    gate_grad_act = (hidden_grad * up_act * silu_slope).astype(jnp.bfloat16)
    up_grad_act = (hidden_grad * silu_act).astype(jnp.bfloat16)
    assign_grad = (jnp.dot(gate_grad_act, gate_weight, preferred_element_type=jnp.float32)
                   + jnp.dot(up_grad_act, up_weight, preferred_element_type=jnp.float32)).astype(jnp.bfloat16)
    gate_weight_grad = inner_first(gate_grad_act, inputs)
    up_weight_grad = inner_first(up_grad_act, inputs)
    down_weight_grad = inner_first(hidden, out_grad)
    out_full = jnp.zeros((TOKENS + 1, D), jnp.bfloat16).at[table].set(expert_out)[:TOKENS]
    grad_full = jnp.zeros((TOKENS + 1, D), jnp.bfloat16).at[table].set(assign_grad)[:TOKENS]
    out_rows = out_full.astype(jnp.float32)
    mixed = (token_gate[:, None] * out_rows).astype(jnp.bfloat16)
    gates_grad = chosen_f * jnp.sum(cotangent.astype(jnp.float32) * out_rows, axis=1)[:, None]
    return (mixed, grad_full, gates_grad, gate_weight_grad, up_weight_grad, down_weight_grad)
```

```python
import jax
import jax.numpy as jnp
from jax import lax
from jax.experimental import pallas as pl
from jax.experimental.pallas import tpu as pltpu
from jax.sharding import PartitionSpec as P

MESH = pl.DeviceIdType.MESH
F32 = jnp.float32
BF16 = jnp.bfloat16
CAP = 20
BLK = 32
NX, NY, NZL = 4, 8, 4
TOK, WID, HID = 128, 384, 128
RA = NY * CAP
RB = NX * CAP
HALF = NX * NY * CAP
OWN = HALF // 8
N_COPIES = 160
VMEM_BYTES = 64 * 1024 * 1024 - 64 * 1024


def dot_nt(a, b):
    return lax.dot_general(a, b, (((1,), (1,)), ((), ())), preferred_element_type=F32)


def dot_tn(a, b):
    return lax.dot_general(a, b, (((0,), (0,)), ((), ())), preferred_element_type=F32)


def dot_nn(a, b):
    return jnp.dot(a, b, preferred_element_type=F32)


def pack_table(blocks):
    rows, cols = blocks * CAP, blocks * BLK
    r = lax.broadcasted_iota(jnp.int32, (rows, cols), 0)
    c = lax.broadcasted_iota(jnp.int32, (rows, cols), 1)
    src = r
    for k in range(1, blocks):
        src = src + jnp.where(r >= k * CAP, BLK - CAP, 0)
    return (src == c).astype(F32).astype(BF16)


def kernel(
    ids_hbm, gates_hbm, tok_hbm, cot_hbm, wg_hbm, wu_hbm, wd_hbm,
    mixed_hbm, tgrad_hbm, ggrad_hbm, dwg_hbm, dwu_hbm, dwd_hbm,
    mixed_ref, tgrad_ref, ggrad_ref, dwg_ref, dwu_ref, dwd_ref,
    ids_ref, gates_ref, tok_ref, cot_ref, wg_ref, wu_ref, wd_ref,
    ga, gb, ina, inb, part, core_in, core_sum, z_in, acts, ea, eb, ra_in, rb_in, rb_far,
    ua, ub, ua_in, ub_in, zo, zo_in, gsum, ta_ref, tb_ref,
    local_sems, send_sems, recv_sems,
):
    d = lax.axis_index("dp")
    g = lax.axis_index("group")
    x = lax.rem(d, NX)
    y = lax.rem(lax.div(d, NX), NY)
    z = lax.div(d, NX * NY)
    core = lax.rem(g, 2)
    zl = lax.div(g, 2)

    def at_x(j):
        return {"dp": z * (NX * NY) + y * NX + lax.rem(x + j, NX)}

    def at_y(j):
        return {"dp": z * (NX * NY) + lax.rem(y + j, NY) * NX + x}

    z_peer = {"dp": (1 - z) * (NX * NY) + y * NX + x}
    core_peer = {"group": zl * 2 + (1 - core)}

    def at_zl(j):
        return {"group": lax.rem(zl + j, NZL) * 2 + core}

    def at_group(j):
        return {"group": lax.rem(g + j, 8)}

    copies = []

    def send(src, dst, device):
        k = len(copies)
        c = pltpu.make_async_remote_copy(
            src_ref=src, dst_ref=dst, send_sem=send_sems.at[k], recv_sem=recv_sems.at[k],
            device_id=device, device_id_type=MESH,
        )
        c.start()
        copies.append(c)
        return c

    def wait_all(cs):
        for c in cs:
            c.wait_recv()

    stores = []

    def keep(src, dst):
        c = pltpu.make_async_copy(src, dst, local_sems.at[7 + len(stores)])
        c.start()
        stores.append(c)

    barrier = pltpu.get_barrier_semaphore()
    partners = [z_peer] + [at_x(j) for j in range(1, NX)] + [at_y(j) for j in range(1, NY)]
    partners += [at_group(j) for j in range(1, 8)]
    for p in partners:
        pl.semaphore_signal(barrier, inc=1, device_id=p, device_id_type=MESH)
    pairs = (
        (ids_hbm, ids_ref), (gates_hbm, gates_ref), (tok_hbm, tok_ref), (cot_hbm, cot_ref),
        (wg_hbm, wg_ref), (wu_hbm, wu_ref), (wd_hbm, wd_ref),
    )
    loads = []
    for i, (src, dst) in enumerate(pairs):
        c = pltpu.make_async_copy(src, dst, local_sems.at[i])
        c.start()
        loads.append(c)
    for c in loads[:4]:
        c.wait()

    chosen = (ids_ref[...] == 0).astype(F32)
    gate_row = jnp.sum(chosen * gates_ref[...], axis=0, keepdims=True)
    picked = jnp.broadcast_to(jnp.max(chosen, axis=0, keepdims=True), (BLK, TOK))
    ri = lax.broadcasted_iota(jnp.int32, (TOK, TOK), 0)
    ci = lax.broadcasted_iota(jnp.int32, (TOK, TOK), 1)
    eye = (ci == ri).astype(F32)
    before = dot_nn(picked.astype(BF16), (ri < ci).astype(F32).astype(BF16))
    slot = lax.broadcasted_iota(jnp.int32, (BLK, TOK), 0)
    hit = jnp.where((before == slot.astype(F32)) & (slot < CAP), picked, 0.0)
    sel = hit.astype(BF16)
    slot_gate = jnp.sum(hit * gate_row, axis=1, keepdims=True)
    ga[0, 0] = dot_nn(sel, tok_ref[...]).astype(BF16)
    ga[1, 0] = (slot_gate * dot_nn(sel, cot_ref[...])).astype(BF16)

    pl.semaphore_wait(barrier, len(partners))

    far_first_y, far_first_x = (4, 3, 5, 2, 6, 1, 7), (2, 1, 3)
    cz, cy = [None, None], [None, None]
    for arr in range(2):
        cz[arr] = send(ga.at[arr, 0], gb.at[arr, 0], z_peer)
        cy[arr] = [send(ga.at[arr, 0], ga.at[arr, j], at_y(j)) for j in far_first_y]
    ta_ref[...] = pack_table(NY)
    tb_ref[...] = pack_table(NX)
    cx = [None, None]
    for arr in range(2):
        cz[arr].wait_recv()
        cx[arr] = [send(gb.at[arr, 0], gb.at[arr, j], at_x(j)) for j in far_first_x]

    def pack(table, blocks):
        n, _, _ = blocks.shape
        return dot_nn(table[...], blocks.reshape(n * BLK, WID)).astype(BF16)

    xa, y_near, y_two, y_far = [None, None], [None, None], [None, None], [None, None]

    def launch_a(arr):
        wait_all(cy[arr])
        ina[arr, 0] = pack(ta_ref, ga[arr])
        xa[arr] = [send(ina.at[arr, 0], ina.at[arr, j], at_x(j)) for j in far_first_x]

    def launch_b(arr):
        wait_all(cx[arr])
        inb[arr, 0] = pack(tb_ref, gb[arr])
        y_two[arr] = [send(inb.at[arr, 0], inb.at[arr, j], at_y(j)) for j in (2, 6)]
        y_near[arr] = [send(inb.at[arr, 0], inb.at[arr, j], at_y(j)) for j in (1, 7)]

    def relay_b(arr):
        out = []
        y_two[arr][0].wait_recv()
        if arr == 0:
            out.append(send(inb.at[arr, 2], inb.at[arr, 4], at_y(2)))
        out.append(send(inb.at[arr, 2], inb.at[arr, 3], at_y(1)))
        y_two[arr][1].wait_recv()
        if arr == 1:
            out.append(send(inb.at[arr, 6], inb.at[arr, 4], at_y(6)))
        out.append(send(inb.at[arr, 6], inb.at[arr, 5], at_y(7)))
        y_far[arr] = out

    launch_a(0)
    launch_b(0)
    launch_a(1)
    launch_b(1)
    relay_b(0)
    relay_b(1)
    for c in loads[4:]:
        c.wait()
    wg, wu, wd = wg_ref[...], wu_ref[...], wd_ref[...]

    def partials(ch, arr, buf):
        rows = buf[arr].reshape(HALF, WID)
        if arr == 0:
            part[ch, 0] = dot_nt(rows, wg).astype(BF16).reshape(8, OWN, HID)
            part[ch, 1] = dot_nt(rows, wu).astype(BF16).reshape(8, OWN, HID)
        else:
            part[ch, 2] = dot_nt(rows, wd).astype(BF16).reshape(8, OWN, HID)
        ks = pl.ds(0, 2) if arr == 0 else pl.ds(2, 1)
        return send(part.at[ch, ks, pl.ds((1 - core) * NZL, NZL)], core_in.at[ch, ks], core_peer)

    def core_reduce(ch, arr, c):
        c.wait_recv()
        ks = pl.ds(0, 2) if arr == 0 else pl.ds(2, 1)
        mine = part[ch, ks, pl.ds(core * NZL, NZL)]
        core_sum[ch, ks] = (mine.astype(F32) + core_in[ch, ks].astype(F32)).astype(BF16)
        return [
            send(core_sum.at[ch, ks, lax.rem(zl + j, NZL)], z_in.at[ch, ks, j - 1], at_zl(j))
            for j in (3, 1, 2)
        ]

    def totals(ch, k):
        tot = core_sum[ch, k, zl].astype(F32)
        for j in range(3):
            tot = tot + z_in[ch, k, j].astype(F32)
        return tot

    own_row = core * NZL + zl

    def share(ch, ks):
        mine = acts.at[ch, ks, own_row]
        cs = {j: send(mine, mine, at_zl(j)) for j in (3, 1, 2)}
        return cs, [send(mine, mine, core_peer)], ks

    def act_forward(ch, cs):
        wait_all(cs)
        gate_act, up_act = totals(ch, 0), totals(ch, 1)
        sig = jax.nn.sigmoid(gate_act)
        silu = gate_act * sig
        acts[ch, 0, own_row] = (silu * up_act).astype(BF16)
        return share(ch, pl.ds(0, 1)), (silu, up_act * (sig * (1.0 + gate_act * (1.0 - sig))))

    def act_backward(ch, cs, kept):
        wait_all(cs)
        hidden_grad = totals(ch, 2)
        acts[ch, 1, own_row] = (hidden_grad * kept[1]).astype(BF16)
        acts[ch, 2, own_row] = (hidden_grad * kept[0]).astype(BF16)
        return share(ch, pl.ds(1, 2))

    def to_core(ch, shared):
        cs, near, ks = shared
        for j in (1, 3, 2):
            cs[j].wait_recv()
            theirs = acts.at[ch, ks, core * NZL + lax.rem(zl + NZL - j, NZL)]
            near.append(send(theirs, theirs, core_peer))
        return near

    wait_all(xa[0])
    core_a0 = partials(0, 0, ina)
    wait_all(y_near[0] + y_far[0])
    core_b0 = partials(1, 0, inb)
    za0 = core_reduce(0, 0, core_a0)
    wait_all(xa[1])
    core_a1 = partials(0, 1, ina)
    zb0 = core_reduce(1, 0, core_b0)
    wait_all(y_near[1] + y_far[1])
    core_b1 = partials(1, 1, inb)
    za1 = core_reduce(0, 1, core_a1)
    zb1 = core_reduce(1, 1, core_b1)
    fa, kept_a = act_forward(0, za0)
    fb, kept_b = act_forward(1, zb0)
    ba = act_backward(0, za1, kept_a)
    bb = act_backward(1, zb1, kept_b)

    def result(ch, arr, near):
        wait_all(near)
        if arr == 0:
            return dot_nn(acts[ch, 0].reshape(HALF, HID), wd).astype(BF16)
        return (
            dot_nn(acts[ch, 1].reshape(HALF, HID), wg) + dot_nn(acts[ch, 2].reshape(HALF, HID), wu)
        ).astype(BF16)

    def back_a(arr, near):
        ea[arr] = result(0, arr, near).reshape(NX, RA, WID)
        xa[arr] = [send(ea.at[arr, k], ra_in.at[arr, k - 1], at_x(NX - k)) for k in (2, 1, 3)]

    def back_b(arr, near):
        eb[arr] = result(1, arr, near).reshape(NY, RB, WID)
        far = 2 if arr == 0 else 6
        y_far[arr] = [
            send(eb.at[arr, 4], rb_far.at[arr, 2], at_y(NY - far)),
            send(eb.at[arr, 3], rb_far.at[arr, 0], at_y(7)),
            send(eb.at[arr, 5], rb_far.at[arr, 1], at_y(1)),
        ]
        y_near[arr] = [
            send(eb.at[arr, 1], rb_in.at[arr, 0], at_y(7)),
            send(eb.at[arr, 7], rb_in.at[arr, 1], at_y(1)),
        ]

    def relay_back_b(arr):
        wait_all(y_far[arr])
        for i, k in enumerate((2, 6)):
            tot = eb[arr, k].astype(F32) + rb_far[arr, i].astype(F32)
            if i == arr:
                tot = tot + rb_far[arr, 2].astype(F32)
            eb[arr, k] = tot.astype(BF16)
            y_near[arr].append(send(eb.at[arr, k], rb_in.at[arr, 2 + i], at_y(NY - k)))

    def unpack(table, tot):
        return dot_tn(table[...], tot.astype(BF16)).astype(BF16)

    def spread_a(arr):
        wait_all(xa[arr])
        tot = ea[arr, 0].astype(F32)
        for j in range(NX - 1):
            tot = tot + ra_in[arr, j].astype(F32)
        ua[arr] = unpack(ta_ref, tot).reshape(NY, BLK, WID)
        cy[arr] = [send(ua.at[arr, k], ua_in.at[arr, k - 1], at_y(NY - k)) for k in far_first_y]

    def spread_b(arr):
        wait_all(y_near[arr])
        tot = eb[arr, 0].astype(F32)
        for j in range(4):
            tot = tot + rb_in[arr, j].astype(F32)
        ub[arr] = unpack(tb_ref, tot).reshape(NX, BLK, WID)
        cx[arr] = [send(ub.at[arr, k], ub_in.at[arr, k - 1], at_x(NX - k)) for k in far_first_x]

    def over_z(arr):
        wait_all(cx[arr])
        tot = ub[arr, 0].astype(F32)
        for j in range(NX - 1):
            tot = tot + ub_in[arr, j].astype(F32)
        zo[arr] = tot.astype(BF16)
        cz[arr] = send(zo.at[arr], zo_in.at[arr], z_peer)

    def final_rows(arr):
        wait_all(cy[arr])
        tot = ua[arr, 0].astype(F32)
        for j in range(NY - 1):
            tot = tot + ua_in[arr, j].astype(F32)
        cz[arr].wait_recv()
        tot = tot + zo_in[arr].astype(F32)
        return dot_tn(sel, tot.astype(BF16))

    def weight_grad(k, arr):
        return dot_tn(acts[0, k].reshape(HALF, HID), ina[arr].reshape(HALF, WID)) + dot_tn(
            acts[1, k].reshape(HALF, HID), inb[arr].reshape(HALF, WID)
        )

    fa = to_core(0, fa)
    fb = to_core(1, fb)
    back_a(0, fa)
    back_b(0, fb)
    ba = to_core(0, ba)
    bb = to_core(1, bb)
    back_b(1, bb)
    back_a(1, ba)
    relay_back_b(0)
    relay_back_b(1)
    dwg_ref[...] = weight_grad(1, 0)
    keep(dwg_ref, dwg_hbm)
    spread_a(0)
    spread_b(0)
    spread_b(1)
    spread_a(1)
    dwu_ref[...] = weight_grad(2, 0)
    keep(dwu_ref, dwu_hbm)
    over_z(0)
    over_z(1)
    dwd_ref[...] = weight_grad(0, 1)
    keep(dwd_ref, dwd_hbm)
    out_rows = final_rows(0)
    gate_term = jnp.sum(cot_ref[...].astype(F32) * out_rows, axis=1, keepdims=True)
    row = jnp.sum(gate_term * eye, axis=0, keepdims=True)
    gsum[g] = jnp.broadcast_to(row, (8, TOK))
    cg = [send(gsum.at[g], gsum.at[g], at_group(j)) for j in (4, 3, 5, 2, 6, 1, 7)]
    token_gate = jnp.sum(eye * gate_row, axis=1, keepdims=True)
    mixed_ref[...] = (token_gate * out_rows).astype(BF16)
    keep(mixed_ref, mixed_hbm)
    tgrad_ref[...] = final_rows(1).astype(BF16)
    keep(tgrad_ref, tgrad_hbm)
    wait_all(cg)
    tot = gsum[0]
    for j in range(1, 8):
        tot = tot + gsum[j]
    ggrad_ref[...] = chosen * tot[0:1]
    keep(ggrad_ref, ggrad_hbm)
    for c in copies:
        c.wait_send()
    for c in stores:
        c.wait()


def store(*refs):
    ins, outs, sems = refs[:6], refs[6:12], refs[12]
    cs = [pltpu.make_async_copy(a, b, sems.at[i]) for i, (a, b) in enumerate(zip(ins, outs))]
    for c in cs:
        c.start()
    for c in cs:
        c.wait()


def on_device(tokens, expert_ids, gates, gate_weight, up_weight, down_weight, cotangent):
    def vm(*shape, kind=BF16):
        return pltpu.VMEM(shape, kind)

    scratch = [
        vm(TOK, WID), vm(TOK, WID), vm(2, TOK, kind=F32),
        vm(HID, WID, kind=F32), vm(HID, WID, kind=F32), vm(HID, WID, kind=F32),
        vm(2, TOK, kind=jnp.int32), vm(2, TOK, kind=F32), vm(TOK, WID), vm(TOK, WID),
        vm(HID, WID), vm(HID, WID), vm(HID, WID),
        vm(2, NY, BLK, WID), vm(2, NX, BLK, WID), vm(2, NX, RA, WID), vm(2, NY, RB, WID),
        vm(2, 3, 8, OWN, HID), vm(2, 3, NZL, OWN, HID), vm(2, 3, NZL, OWN, HID),
        vm(2, 3, 3, OWN, HID), vm(2, 3, 8, OWN, HID),
        vm(2, NX, RA, WID), vm(2, NY, RB, WID), vm(2, 3, RA, WID), vm(2, 4, RB, WID), vm(2, 3, RB, WID),
        vm(2, NY, BLK, WID), vm(2, NX, BLK, WID), vm(2, NY - 1, BLK, WID), vm(2, NX - 1, BLK, WID),
        vm(2, BLK, WID), vm(2, BLK, WID), vm(8, 8, TOK, kind=F32),
        vm(RA, NY * BLK), vm(RB, NX * BLK),
        pltpu.SemaphoreType.DMA((13,)),
        pltpu.SemaphoreType.DMA((N_COPIES,)), pltpu.SemaphoreType.DMA((N_COPIES,)),
    ]
    half = jax.ShapeDtypeStruct((TOK, WID), BF16)
    full = jax.ShapeDtypeStruct((TOK, WID), F32)
    shapes = (half, half, jax.ShapeDtypeStruct((2, TOK), F32), full, full, full)
    results = pl.pallas_call(
        kernel,
        out_shape=shapes,
        in_specs=[pl.BlockSpec(memory_space=pl.ANY)] * 7,
        out_specs=[pl.BlockSpec(memory_space=pl.ANY)] * 6,
        scratch_shapes=scratch,
        compiler_params=pltpu.CompilerParams(
            collective_id=0, has_side_effects=True, vmem_limit_bytes=VMEM_BYTES
        ),
    )(expert_ids.T, gates.T, tokens, cotangent, gate_weight, up_weight, down_weight)
    mixed, tgrad, ggrad, dwg, dwu, dwd = pl.pallas_call(
        store,
        out_shape=shapes,
        in_specs=[pl.BlockSpec(memory_space=pl.ANY)] * 6,
        out_specs=[pl.BlockSpec(memory_space=pl.ANY)] * 6,
        scratch_shapes=[pltpu.SemaphoreType.DMA((6,))],
        compiler_params=pltpu.CompilerParams(vmem_limit_bytes=VMEM_BYTES),
    )(*results)
    return mixed, tgrad, ggrad.T, dwg, dwu, dwd


def solution(mesh):
    wide, narrow = P("dp", "group"), P("dp", None)
    return jax.shard_map(
        on_device,
        mesh=mesh,
        in_specs=(wide, narrow, narrow, wide, wide, wide, wide),
        out_specs=(wide, wide, narrow, wide, wide, wide),
        check_vma=False,
    )
```

```python
import jax
import jax.numpy as jnp
from jax import lax
from jax.experimental import pallas as pl
from jax.experimental.pallas import tpu as pltpu
from jax.sharding import PartitionSpec as P

MESH = pl.DeviceIdType.MESH
F32 = jnp.float32
BF16 = jnp.bfloat16
CAP = 20
BLK = 32
NX, NY, NZL = 4, 8, 4
TOK, WID, HID = 128, 384, 128
RA = NY * CAP
RB = NX * CAP
HALF = NX * NY * CAP
OWN = HALF // 8
N_COPIES = 160
VMEM_BYTES = 64 * 1024 * 1024 - 64 * 1024


def dot_nt(a, b):
    return lax.dot_general(a, b, (((1,), (1,)), ((), ())), preferred_element_type=F32)


def dot_tn(a, b):
    return lax.dot_general(a, b, (((0,), (0,)), ((), ())), preferred_element_type=F32)


def dot_nn(a, b):
    return jnp.dot(a, b, preferred_element_type=F32)


def pack_table(blocks):
    rows, cols = blocks * CAP, blocks * BLK
    r = lax.broadcasted_iota(jnp.int32, (rows, cols), 0)
    c = lax.broadcasted_iota(jnp.int32, (rows, cols), 1)
    src = r
    for k in range(1, blocks):
        src = src + jnp.where(r >= k * CAP, BLK - CAP, 0)
    return (src == c).astype(F32).astype(BF16)


def kernel(
    ids_hbm, gates_hbm, tok_hbm, cot_hbm, wg_hbm, wu_hbm, wd_hbm,
    mixed_hbm, tgrad_hbm, ggrad_hbm, dwg_hbm, dwu_hbm, dwd_hbm,
    mixed_ref, tgrad_ref, ggrad_ref, dwg_ref, dwu_ref, dwd_ref,
    ids_ref, gates_ref, tok_ref, cot_ref, wg_ref, wu_ref, wd_ref,
    ga, gb, ina, inb, part, core_in, core_sum, z_in, acts, ea, eb, ra_in, rb_in, rb_far,
    ua, ub, ua_in, ub_in, zo, zo_in, gsum, ta_ref, tb_ref,
    local_sems, send_sems, recv_sems,
):
    d = lax.axis_index("dp")
    g = lax.axis_index("group")
    x = lax.rem(d, NX)
    y = lax.rem(lax.div(d, NX), NY)
    z = lax.div(d, NX * NY)
    core = lax.rem(g, 2)
    zl = lax.div(g, 2)

    def at_x(j):
        return {"dp": z * (NX * NY) + y * NX + lax.rem(x + j, NX)}

    def at_y(j):
        return {"dp": z * (NX * NY) + lax.rem(y + j, NY) * NX + x}

    z_peer = {"dp": (1 - z) * (NX * NY) + y * NX + x}
    core_peer = {"group": zl * 2 + (1 - core)}

    def at_zl(j):
        return {"group": lax.rem(zl + j, NZL) * 2 + core}

    def at_group(j):
        return {"group": lax.rem(g + j, 8)}

    copies = []

    def send(src, dst, device):
        k = len(copies)
        c = pltpu.make_async_remote_copy(
            src_ref=src, dst_ref=dst, send_sem=send_sems.at[k], recv_sem=recv_sems.at[k],
            device_id=device, device_id_type=MESH,
        )
        c.start()
        copies.append(c)
        return c

    def wait_all(cs):
        for c in cs:
            c.wait_recv()

    stores = []

    def keep(src, dst):
        c = pltpu.make_async_copy(src, dst, local_sems.at[7 + len(stores)])
        c.start()
        stores.append(c)

    barrier = pltpu.get_barrier_semaphore()
    partners = [z_peer] + [at_x(j) for j in range(1, NX)] + [at_y(j) for j in range(1, NY)]
    partners += [at_group(j) for j in range(1, 8)]
    for p in partners:
        pl.semaphore_signal(barrier, inc=1, device_id=p, device_id_type=MESH)
    pairs = (
        (ids_hbm, ids_ref), (gates_hbm, gates_ref), (tok_hbm, tok_ref), (cot_hbm, cot_ref),
        (wg_hbm, wg_ref), (wu_hbm, wu_ref), (wd_hbm, wd_ref),
    )
    loads = []
    for i, (src, dst) in enumerate(pairs):
        c = pltpu.make_async_copy(src, dst, local_sems.at[i])
        c.start()
        loads.append(c)
    for c in loads[:4]:
        c.wait()

    chosen = (ids_ref[...] == 0).astype(F32)
    gate_row = jnp.sum(chosen * gates_ref[...], axis=0, keepdims=True)
    picked = jnp.broadcast_to(jnp.max(chosen, axis=0, keepdims=True), (BLK, TOK))
    ri = lax.broadcasted_iota(jnp.int32, (TOK, TOK), 0)
    ci = lax.broadcasted_iota(jnp.int32, (TOK, TOK), 1)
    eye = (ci == ri).astype(F32)
    before = dot_nn(picked.astype(BF16), (ri < ci).astype(F32).astype(BF16))
    slot = lax.broadcasted_iota(jnp.int32, (BLK, TOK), 0)
    hit = jnp.where((before == slot.astype(F32)) & (slot < CAP), picked, 0.0)
    sel = hit.astype(BF16)
    slot_gate = jnp.sum(hit * gate_row, axis=1, keepdims=True)
    ga[0, 0] = dot_nn(sel, tok_ref[...]).astype(BF16)
    ga[1, 0] = (slot_gate * dot_nn(sel, cot_ref[...])).astype(BF16)

    pl.semaphore_wait(barrier, len(partners))

    far_first_y, far_first_x = (4, 3, 5, 2, 6, 1, 7), (2, 1, 3)
    cz, cy = [None, None], [None, None]
    for arr in range(2):
        cz[arr] = send(ga.at[arr, 0], gb.at[arr, 0], z_peer)
        cy[arr] = [send(ga.at[arr, 0], ga.at[arr, j], at_y(j)) for j in far_first_y]
    ta_ref[...] = pack_table(NY)
    tb_ref[...] = pack_table(NX)
    cx = [None, None]
    for arr in range(2):
        cz[arr].wait_recv()
        cx[arr] = [send(gb.at[arr, 0], gb.at[arr, j], at_x(j)) for j in far_first_x]

    def pack(table, blocks):
        n, _, _ = blocks.shape
        return dot_nn(table[...], blocks.reshape(n * BLK, WID)).astype(BF16)

    xa, y_near, y_two, y_far = [None, None], [None, None], [None, None], [None, None]

    def launch_a(arr):
        wait_all(cy[arr])
        ina[arr, 0] = pack(ta_ref, ga[arr])
        xa[arr] = [send(ina.at[arr, 0], ina.at[arr, j], at_x(j)) for j in far_first_x]

    def launch_b(arr):
        wait_all(cx[arr])
        inb[arr, 0] = pack(tb_ref, gb[arr])
        y_two[arr] = [send(inb.at[arr, 0], inb.at[arr, j], at_y(j)) for j in (2, 6)]
        y_near[arr] = [send(inb.at[arr, 0], inb.at[arr, j], at_y(j)) for j in (1, 7)]

    def relay_b(arr):
        out = []
        y_two[arr][0].wait_recv()
        if arr == 0:
            out.append(send(inb.at[arr, 2], inb.at[arr, 4], at_y(2)))
        out.append(send(inb.at[arr, 2], inb.at[arr, 3], at_y(1)))
        y_two[arr][1].wait_recv()
        if arr == 1:
            out.append(send(inb.at[arr, 6], inb.at[arr, 4], at_y(6)))
        out.append(send(inb.at[arr, 6], inb.at[arr, 5], at_y(7)))
        y_far[arr] = out

    launch_a(0)
    launch_b(0)
    launch_a(1)
    launch_b(1)
    relay_b(0)
    relay_b(1)
    for c in loads[4:]:
        c.wait()
    wg, wu, wd = wg_ref[...], wu_ref[...], wd_ref[...]

    def partials(ch, arr, buf):
        rows = buf[arr].reshape(HALF, WID)
        if arr == 0:
            part[ch, 0] = dot_nt(rows, wg).astype(BF16).reshape(8, OWN, HID)
            part[ch, 1] = dot_nt(rows, wu).astype(BF16).reshape(8, OWN, HID)
        else:
            part[ch, 2] = dot_nt(rows, wd).astype(BF16).reshape(8, OWN, HID)
        ks = pl.ds(0, 2) if arr == 0 else pl.ds(2, 1)
        return send(part.at[ch, ks, pl.ds((1 - core) * NZL, NZL)], core_in.at[ch, ks], core_peer)

    def core_reduce(ch, arr, c):
        c.wait_recv()
        ks = pl.ds(0, 2) if arr == 0 else pl.ds(2, 1)
        mine = part[ch, ks, pl.ds(core * NZL, NZL)]
        core_sum[ch, ks] = (mine.astype(F32) + core_in[ch, ks].astype(F32)).astype(BF16)
        return [
            send(core_sum.at[ch, ks, lax.rem(zl + j, NZL)], z_in.at[ch, ks, j - 1], at_zl(j))
            for j in (3, 1, 2)
        ]

    def totals(ch, k):
        tot = core_sum[ch, k, zl].astype(F32)
        for j in range(3):
            tot = tot + z_in[ch, k, j].astype(F32)
        return tot

    own_row = core * NZL + zl

    def share(ch, ks):
        mine = acts.at[ch, ks, own_row]
        cs = {j: send(mine, mine, at_zl(j)) for j in (3, 1, 2)}
        return cs, [send(mine, mine, core_peer)], ks

    def act_forward(ch, cs):
        wait_all(cs)
        gate_act, up_act = totals(ch, 0), totals(ch, 1)
        sig = jax.nn.sigmoid(gate_act)
        silu = gate_act * sig
        acts[ch, 0, own_row] = (silu * up_act).astype(BF16)
        return share(ch, pl.ds(0, 1)), (silu, up_act * (sig * (1.0 + gate_act * (1.0 - sig))))

    def act_backward(ch, cs, kept):
        wait_all(cs)
        hidden_grad = totals(ch, 2)
        acts[ch, 1, own_row] = (hidden_grad * kept[1]).astype(BF16)
        acts[ch, 2, own_row] = (hidden_grad * kept[0]).astype(BF16)
        return share(ch, pl.ds(1, 2))

    def to_core(ch, shared):
        cs, near, ks = shared
        for j in (1, 3, 2):
            cs[j].wait_recv()
            theirs = acts.at[ch, ks, core * NZL + lax.rem(zl + NZL - j, NZL)]
            near.append(send(theirs, theirs, core_peer))
        return near

    wait_all(xa[0])
    core_a0 = partials(0, 0, ina)
    wait_all(y_near[0] + y_far[0])
    core_b0 = partials(1, 0, inb)
    za0 = core_reduce(0, 0, core_a0)
    wait_all(xa[1])
    core_a1 = partials(0, 1, ina)
    zb0 = core_reduce(1, 0, core_b0)
    wait_all(y_near[1] + y_far[1])
    core_b1 = partials(1, 1, inb)
    za1 = core_reduce(0, 1, core_a1)
    zb1 = core_reduce(1, 1, core_b1)
    fa, kept_a = act_forward(0, za0)
    fb, kept_b = act_forward(1, zb0)
    ba = act_backward(0, za1, kept_a)
    bb = act_backward(1, zb1, kept_b)

    def result(ch, arr, near):
        wait_all(near)
        if arr == 0:
            return dot_nn(acts[ch, 0].reshape(HALF, HID), wd).astype(BF16)
        return (
            dot_nn(acts[ch, 1].reshape(HALF, HID), wg) + dot_nn(acts[ch, 2].reshape(HALF, HID), wu)
        ).astype(BF16)

    def back_a(arr, near):
        ea[arr] = result(0, arr, near).reshape(NX, RA, WID)
        xa[arr] = [send(ea.at[arr, k], ra_in.at[arr, k - 1], at_x(NX - k)) for k in (2, 1, 3)]

    def back_b(arr, near):
        eb[arr] = result(1, arr, near).reshape(NY, RB, WID)
        far = 2 if arr == 0 else 6
        y_far[arr] = [
            send(eb.at[arr, 4], rb_far.at[arr, 2], at_y(NY - far)),
            send(eb.at[arr, 3], rb_far.at[arr, 0], at_y(7)),
            send(eb.at[arr, 5], rb_far.at[arr, 1], at_y(1)),
        ]
        y_near[arr] = [
            send(eb.at[arr, 1], rb_in.at[arr, 0], at_y(7)),
            send(eb.at[arr, 7], rb_in.at[arr, 1], at_y(1)),
        ]

    def relay_back_b(arr):
        wait_all(y_far[arr])
        for i, k in enumerate((2, 6)):
            tot = eb[arr, k].astype(F32) + rb_far[arr, i].astype(F32)
            if i == arr:
                tot = tot + rb_far[arr, 2].astype(F32)
            eb[arr, k] = tot.astype(BF16)
            y_near[arr].append(send(eb.at[arr, k], rb_in.at[arr, 2 + i], at_y(NY - k)))

    def unpack(table, tot):
        return dot_tn(table[...], tot.astype(BF16)).astype(BF16)

    def spread_a(arr):
        wait_all(xa[arr])
        tot = ea[arr, 0].astype(F32)
        for j in range(NX - 1):
            tot = tot + ra_in[arr, j].astype(F32)
        ua[arr] = unpack(ta_ref, tot).reshape(NY, BLK, WID)
        cy[arr] = [send(ua.at[arr, k], ua_in.at[arr, k - 1], at_y(NY - k)) for k in far_first_y]

    def spread_b(arr):
        wait_all(y_near[arr])
        tot = eb[arr, 0].astype(F32)
        for j in range(4):
            tot = tot + rb_in[arr, j].astype(F32)
        ub[arr] = unpack(tb_ref, tot).reshape(NX, BLK, WID)
        cx[arr] = [send(ub.at[arr, k], ub_in.at[arr, k - 1], at_x(NX - k)) for k in far_first_x]

    def over_z(arr):
        wait_all(cx[arr])
        tot = ub[arr, 0].astype(F32)
        for j in range(NX - 1):
            tot = tot + ub_in[arr, j].astype(F32)
        zo[arr] = tot.astype(BF16)
        cz[arr] = send(zo.at[arr], zo_in.at[arr], z_peer)

    def final_rows(arr):
        wait_all(cy[arr])
        tot = ua[arr, 0].astype(F32)
        for j in range(NY - 1):
            tot = tot + ua_in[arr, j].astype(F32)
        cz[arr].wait_recv()
        tot = tot + zo_in[arr].astype(F32)
        return dot_tn(sel, tot.astype(BF16))

    def weight_grad(k, arr):
        return dot_tn(acts[0, k].reshape(HALF, HID), ina[arr].reshape(HALF, WID)) + dot_tn(
            acts[1, k].reshape(HALF, HID), inb[arr].reshape(HALF, WID)
        )

    fa = to_core(0, fa)
    fb = to_core(1, fb)
    back_a(0, fa)
    back_b(0, fb)
    ba = to_core(0, ba)
    bb = to_core(1, bb)
    back_b(1, bb)
    back_a(1, ba)
    relay_back_b(0)
    relay_back_b(1)
    dwg_ref[...] = weight_grad(1, 0)
    keep(dwg_ref, dwg_hbm)
    spread_a(0)
    spread_b(0)
    spread_b(1)
    spread_a(1)
    dwu_ref[...] = weight_grad(2, 0)
    keep(dwu_ref, dwu_hbm)
    over_z(0)
    over_z(1)
    dwd_ref[...] = weight_grad(0, 1)
    keep(dwd_ref, dwd_hbm)
    out_rows = final_rows(0)
    gate_term = jnp.sum(cot_ref[...].astype(F32) * out_rows, axis=1, keepdims=True)
    row = jnp.sum(gate_term * eye, axis=0, keepdims=True)
    gsum[g] = jnp.broadcast_to(row, (8, TOK))
    cg = [send(gsum.at[g], gsum.at[g], at_group(j)) for j in (4, 3, 5, 2, 6, 1, 7)]
    token_gate = jnp.sum(eye * gate_row, axis=1, keepdims=True)
    mixed_ref[...] = (token_gate * out_rows).astype(BF16)
    keep(mixed_ref, mixed_hbm)
    tgrad_ref[...] = final_rows(1).astype(BF16)
    keep(tgrad_ref, tgrad_hbm)
    wait_all(cg)
    tot = gsum[0]
    for j in range(1, 8):
        tot = tot + gsum[j]
    ggrad_ref[...] = chosen * tot[0:1]
    keep(ggrad_ref, ggrad_hbm)
    for c in copies:
        c.wait_send()
    for c in stores:
        c.wait()


def store(*refs):
    ins, outs, mids, in_sems, out_sems = refs[:6], refs[6:12], refs[12:18], refs[18], refs[19]
    loads = [pltpu.make_async_copy(a, m, in_sems.at[i]) for i, (a, m) in enumerate(zip(ins, mids))]
    saves = [pltpu.make_async_copy(m, b, out_sems.at[i]) for i, (m, b) in enumerate(zip(mids, outs))]
    for c in loads:
        c.start()
    for load, save in zip(loads, saves):
        load.wait()
        save.start()
    for c in saves:
        c.wait()


def on_device(tokens, expert_ids, gates, gate_weight, up_weight, down_weight, cotangent):
    def vm(*shape, kind=BF16):
        return pltpu.VMEM(shape, kind)

    scratch = [
        vm(TOK, WID), vm(TOK, WID), vm(2, TOK, kind=F32),
        vm(HID, WID, kind=F32), vm(HID, WID, kind=F32), vm(HID, WID, kind=F32),
        vm(2, TOK, kind=jnp.int32), vm(2, TOK, kind=F32), vm(TOK, WID), vm(TOK, WID),
        vm(HID, WID), vm(HID, WID), vm(HID, WID),
        vm(2, NY, BLK, WID), vm(2, NX, BLK, WID), vm(2, NX, RA, WID), vm(2, NY, RB, WID),
        vm(2, 3, 8, OWN, HID), vm(2, 3, NZL, OWN, HID), vm(2, 3, NZL, OWN, HID),
        vm(2, 3, 3, OWN, HID), vm(2, 3, 8, OWN, HID),
        vm(2, NX, RA, WID), vm(2, NY, RB, WID), vm(2, 3, RA, WID), vm(2, 4, RB, WID), vm(2, 3, RB, WID),
        vm(2, NY, BLK, WID), vm(2, NX, BLK, WID), vm(2, NY - 1, BLK, WID), vm(2, NX - 1, BLK, WID),
        vm(2, BLK, WID), vm(2, BLK, WID), vm(8, 8, TOK, kind=F32),
        vm(RA, NY * BLK), vm(RB, NX * BLK),
        pltpu.SemaphoreType.DMA((13,)),
        pltpu.SemaphoreType.DMA((N_COPIES,)), pltpu.SemaphoreType.DMA((N_COPIES,)),
    ]
    half = jax.ShapeDtypeStruct((TOK, WID), BF16)
    full = jax.ShapeDtypeStruct((TOK, WID), F32)
    shapes = (half, half, jax.ShapeDtypeStruct((2, TOK), F32), full, full, full)
    results = pl.pallas_call(
        kernel,
        out_shape=shapes,
        in_specs=[pl.BlockSpec(memory_space=pl.ANY)] * 7,
        out_specs=[pl.BlockSpec(memory_space=pl.ANY)] * 6,
        scratch_shapes=scratch,
        compiler_params=pltpu.CompilerParams(
            collective_id=0, has_side_effects=True, vmem_limit_bytes=VMEM_BYTES
        ),
    )(expert_ids.T, gates.T, tokens, cotangent, gate_weight, up_weight, down_weight)
    mixed, tgrad, ggrad, dwg, dwu, dwd = pl.pallas_call(
        store,
        out_shape=shapes,
        in_specs=[pl.BlockSpec(memory_space=pl.ANY)] * 6,
        out_specs=[pl.BlockSpec(memory_space=pl.ANY)] * 6,
        scratch_shapes=scratch[:6] + [pltpu.SemaphoreType.DMA((6,))] * 2,
        compiler_params=pltpu.CompilerParams(vmem_limit_bytes=VMEM_BYTES),
    )(*results)
    return mixed, tgrad, ggrad.T, dwg, dwu, dwd


def solution(mesh):
    wide, narrow = P("dp", "group"), P("dp", None)
    return jax.shard_map(
        on_device,
        mesh=mesh,
        in_specs=(wide, narrow, narrow, wide, wide, wide, wide),
        out_specs=(wide, wide, narrow, wide, wide, wide),
        check_vma=False,
    )
```

```python
import jax
import jax.numpy as jnp
from jax import lax
from jax.experimental import pallas as pl
from jax.experimental.pallas import tpu as pltpu
from jax.sharding import PartitionSpec as P

MESH = pl.DeviceIdType.MESH
F32 = jnp.float32
BF16 = jnp.bfloat16
CAP = 20
BLK = 32
NX, NY, NZL = 4, 8, 4
TOK, WID, HID = 128, 384, 128
RA = NY * CAP
RB = NX * CAP
HALF = NX * NY * CAP
OWN = HALF // 8
RB_CUT = 48
N_COPIES = 192
VMEM_BYTES = 64 * 1024 * 1024 - 64 * 1024


def dot_nt(a, b):
    return lax.dot_general(a, b, (((1,), (1,)), ((), ())), preferred_element_type=F32)


def dot_tn(a, b):
    return lax.dot_general(a, b, (((0,), (0,)), ((), ())), preferred_element_type=F32)


def dot_nn(a, b):
    return jnp.dot(a, b, preferred_element_type=F32)


def pack_table(blocks):
    rows, cols = blocks * CAP, blocks * BLK
    r = lax.broadcasted_iota(jnp.int32, (rows, cols), 0)
    c = lax.broadcasted_iota(jnp.int32, (rows, cols), 1)
    src = r
    for k in range(1, blocks):
        src = src + jnp.where(r >= k * CAP, BLK - CAP, 0)
    return (src == c).astype(F32).astype(BF16)


def order_table():
    r = lax.broadcasted_iota(jnp.int32, (HALF, TOK), 0)
    y = jnp.zeros_like(r)
    for k in range(1, NY):
        y = y + (r >= k * RB).astype(jnp.int32)
    x, q = jnp.zeros_like(r), r - y * RB
    for k in range(1, NX):
        x = x + (q >= k * CAP).astype(jnp.int32)
    src = x * RA + y * CAP + q - x * CAP
    c = lax.broadcasted_iota(jnp.int32, (HALF, TOK), 1)
    return jnp.concatenate(
        [(src == c + k * TOK).astype(F32).astype(BF16) for k in range(HALF // TOK)], axis=1
    )


def kernel(
    ids_hbm, gates_hbm, tok_hbm, cot_hbm, wg_hbm, wu_hbm, wd_hbm,
    mixed_hbm, tgrad_hbm, ggrad_hbm, dwg_hbm, dwu_hbm, dwd_hbm,
    mixed_ref, tgrad_ref, ggrad_ref, dwg_ref, dwu_ref, dwd_ref,
    ids_ref, gates_ref, tok_ref, cot_ref, wg_ref, wu_ref, wd_ref,
    g8, g4, big4, big8, ordered, part, core_in, core_sum, z_in, acts,
    e4, x_in, x_far, e8, y_in_big, y_far_big, y_half_big, u8, y_in8, y_far8, y_half8, u4, u4_in,
    zo, zo_in, gsum, ta_ref, tb_ref, perm_ref,
    local_sems, send_sems, recv_sems,
):
    d = lax.axis_index("dp")
    g = lax.axis_index("group")
    x = lax.rem(d, NX)
    y = lax.rem(lax.div(d, NX), NY)
    z = lax.div(d, NX * NY)
    core = lax.rem(g, 2)
    zl = lax.div(g, 2)

    def at_x(j):
        return {"dp": z * (NX * NY) + y * NX + lax.rem(x + j, NX)}

    def at_y(j):
        return {"dp": z * (NX * NY) + lax.rem(y + j, NY) * NX + x}

    z_peer = {"dp": (1 - z) * (NX * NY) + y * NX + x}
    core_peer = {"group": zl * 2 + (1 - core)}

    def at_zl(j):
        return {"group": lax.rem(zl + j, NZL) * 2 + core}

    def at_group(j):
        return {"group": lax.rem(g + j, 8)}

    copies = []

    def send(src, dst, device):
        k = len(copies)
        c = pltpu.make_async_remote_copy(
            src_ref=src, dst_ref=dst, send_sem=send_sems.at[k], recv_sem=recv_sems.at[k],
            device_id=device, device_id_type=MESH,
        )
        c.start()
        copies.append(c)
        return c

    def wait_all(cs):
        for c in cs:
            c.wait_recv()

    stores = []

    def keep(src, dst):
        c = pltpu.make_async_copy(src, dst, local_sems.at[7 + len(stores)])
        c.start()
        stores.append(c)

    barrier = pltpu.get_barrier_semaphore()
    partners = [z_peer] + [at_x(j) for j in range(1, NX)] + [at_y(j) for j in range(1, NY)]
    partners += [at_group(j) for j in range(1, 8)]
    for p in partners:
        pl.semaphore_signal(barrier, inc=1, device_id=p, device_id_type=MESH)
    pairs = (
        (ids_hbm, ids_ref), (gates_hbm, gates_ref), (tok_hbm, tok_ref), (cot_hbm, cot_ref),
        (wg_hbm, wg_ref), (wu_hbm, wu_ref), (wd_hbm, wd_ref),
    )
    loads = []
    for i, (src, dst) in enumerate(pairs):
        c = pltpu.make_async_copy(src, dst, local_sems.at[i])
        c.start()
        loads.append(c)
    for c in loads[:4]:
        c.wait()

    chosen = (ids_ref[...] == 0).astype(F32)
    gate_row = jnp.sum(chosen * gates_ref[...], axis=0, keepdims=True)
    picked = jnp.broadcast_to(jnp.max(chosen, axis=0, keepdims=True), (BLK, TOK))
    ri = lax.broadcasted_iota(jnp.int32, (TOK, TOK), 0)
    ci = lax.broadcasted_iota(jnp.int32, (TOK, TOK), 1)
    eye = (ci == ri).astype(F32)
    before = dot_nn(picked.astype(BF16), (ri < ci).astype(F32).astype(BF16))
    slot = lax.broadcasted_iota(jnp.int32, (BLK, TOK), 0)
    hit = jnp.where((before == slot.astype(F32)) & (slot < CAP), picked, 0.0)
    sel = hit.astype(BF16)
    slot_gate = jnp.sum(hit * gate_row, axis=1, keepdims=True)
    g8[0, 0] = dot_nn(sel, tok_ref[...]).astype(BF16)
    g8[1, 0] = (slot_gate * dot_nn(sel, cot_ref[...])).astype(BF16)

    pl.semaphore_wait(barrier, len(partners))

    def y_start(buf):
        two = [send(buf.at[0], buf.at[j], at_y(j)) for j in (2, 6)]
        return two, [send(buf.at[0], buf.at[j], at_y(j)) for j in (1, 7)]

    def y_relay(buf, cut, started):
        two, rest = started
        n = buf.shape[1]
        lo, hi = pl.ds(0, cut), pl.ds(cut, n - cut)
        two[0].wait_recv()
        rest.append(send(buf.at[2, lo], buf.at[4, lo], at_y(2)))
        rest.append(send(buf.at[2], buf.at[3], at_y(1)))
        two[1].wait_recv()
        rest.append(send(buf.at[6, hi], buf.at[4, hi], at_y(6)))
        rest.append(send(buf.at[6], buf.at[5], at_y(7)))
        return rest

    x_lo, x_hi = pl.ds(0, RA // 2), pl.ds(RA // 2, RA // 2)

    def x_start(buf):
        first = [send(buf.at[0, x_lo], buf.at[1, x_lo], at_x(1)), send(buf.at[0, x_hi], buf.at[3, x_hi], at_x(3))]
        return first, [
            send(buf.at[0, x_hi], buf.at[1, x_hi], at_x(1)), send(buf.at[0, x_lo], buf.at[3, x_lo], at_x(3))
        ]

    def x_relay(buf, started):
        first, rest = started
        first[0].wait_recv()
        rest.append(send(buf.at[1, x_lo], buf.at[2, x_lo], at_x(1)))
        first[1].wait_recv()
        rest.append(send(buf.at[3, x_hi], buf.at[2, x_hi], at_x(3)))
        return rest

    def pack(table, blocks):
        n, _, _ = blocks.shape
        return dot_nn(table[...], blocks.reshape(n * BLK, WID)).astype(BF16)

    far_first_x = (2, 1, 3)
    small = [g8.at[q] for q in range(3)]
    big = [big4.at[q] for q in range(3)]
    cz_tok = send(g8.at[0, 0], g4.at[0], z_peer)
    cz_grad = send(g8.at[1, 0], g8.at[2, 0], z_peer)
    ys = [y_start(small[0]), y_start(small[1]), None]
    ta_ref[...] = pack_table(NY)
    tb_ref[...] = pack_table(NX)
    cz_tok.wait_recv()
    cx = [send(g4.at[0], g4.at[j], at_x(j)) for j in far_first_x]
    cz_grad.wait_recv()
    ys[2] = y_start(small[2])
    for q in range(2):
        ys[q] = y_relay(small[q], BLK // 2, ys[q])
    wait_all(cx)
    big8[0] = pack(tb_ref, g4[...])
    y_big = y_start(big8)

    def launch_x(q):
        wait_all(ys[q])
        big4[q, 0] = pack(ta_ref, g8[q])
        return x_start(big[q])

    xs = [launch_x(0), launch_x(1), None]
    ys[2] = y_relay(small[2], BLK // 2, ys[2])
    y_big = y_relay(big8, RB_CUT, y_big)
    perm_ref[...] = order_table()
    xs[0] = x_relay(big[0], xs[0])
    xs[2] = launch_x(2)
    xs[1] = x_relay(big[1], xs[1])
    for c in loads[4:]:
        c.wait()
    wg, wu, wd = wg_ref[...], wu_ref[...], wd_ref[...]

    def partials(ch, arr, rows):
        if arr == 0:
            part[ch, 0] = dot_nt(rows, wg).astype(BF16).reshape(8, OWN, HID)
            part[ch, 1] = dot_nt(rows, wu).astype(BF16).reshape(8, OWN, HID)
        else:
            part[ch, 2] = dot_nt(rows, wd).astype(BF16).reshape(8, OWN, HID)
        ks = pl.ds(0, 2) if arr == 0 else pl.ds(2, 1)
        return send(part.at[ch, ks, pl.ds((1 - core) * NZL, NZL)], core_in.at[ch, ks], core_peer)

    def core_reduce(ch, arr, c):
        c.wait_recv()
        ks = pl.ds(0, 2) if arr == 0 else pl.ds(2, 1)
        mine = part[ch, ks, pl.ds(core * NZL, NZL)]
        core_sum[ch, ks] = (mine.astype(F32) + core_in[ch, ks].astype(F32)).astype(BF16)
        return [
            send(core_sum.at[ch, ks, lax.rem(zl + j, NZL)], z_in.at[ch, ks, j - 1], at_zl(j))
            for j in (3, 1, 2)
        ]

    def totals(ch, k):
        tot = core_sum[ch, k, zl].astype(F32)
        for j in range(3):
            tot = tot + z_in[ch, k, j].astype(F32)
        return tot

    own_row = core * NZL + zl

    def share(ch, ks):
        mine = acts.at[ch, ks, own_row]
        cs = {j: send(mine, mine, at_zl(j)) for j in (3, 1, 2)}
        return cs, [send(mine, mine, core_peer)], ks

    def act_forward(ch, cs):
        wait_all(cs)
        gate_act, up_act = totals(ch, 0), totals(ch, 1)
        sig = jax.nn.sigmoid(gate_act)
        silu = gate_act * sig
        acts[ch, 0, own_row] = (silu * up_act).astype(BF16)
        return share(ch, pl.ds(0, 1)), (silu, up_act * (sig * (1.0 + gate_act * (1.0 - sig))))

    def act_backward(ch, cs, kept):
        wait_all(cs)
        hidden_grad = totals(ch, 2)
        acts[ch, 1, own_row] = (hidden_grad * kept[1]).astype(BF16)
        acts[ch, 2, own_row] = (hidden_grad * kept[0]).astype(BF16)
        return share(ch, pl.ds(1, 2))

    def to_core(ch, shared):
        cs, near, ks = shared
        for j in (1, 3, 2):
            cs[j].wait_recv()
            theirs = acts.at[ch, ks, core * NZL + lax.rem(zl + NZL - j, NZL)]
            near.append(send(theirs, theirs, core_peer))
        return near

    def rows_of(name):
        if name == "other tokens":
            return big8[...].reshape(HALF, WID)
        if name == "other grads":
            return ordered[...]
        return big4[0 if name == "own tokens" else 1].reshape(HALF, WID)

    wait_all(xs[0])
    core_a0 = partials(0, 0, rows_of("own tokens"))
    xs[2] = x_relay(big[2], xs[2])
    wait_all(y_big)
    core_b0 = partials(1, 0, rows_of("other tokens"))
    za0 = core_reduce(0, 0, core_a0)
    wait_all(xs[1])
    core_a1 = partials(0, 1, rows_of("own grads"))
    zb0 = core_reduce(1, 0, core_b0)
    wait_all(xs[2])
    ordered[...] = dot_nn(perm_ref[...], big4[2].reshape(HALF, WID)).astype(BF16)
    core_b1 = partials(1, 1, rows_of("other grads"))
    za1 = core_reduce(0, 1, core_a1)
    zb1 = core_reduce(1, 1, core_b1)
    fa, kept_a = act_forward(0, za0)
    fb, kept_b = act_forward(1, zb0)
    ba = act_backward(0, za1, kept_a)
    bb = act_backward(1, zb1, kept_b)

    def result(ch, arr, near):
        wait_all(near)
        if arr == 0:
            return dot_nn(acts[ch, 0].reshape(HALF, HID), wd).astype(BF16)
        return (
            dot_nn(acts[ch, 1].reshape(HALF, HID), wg) + dot_nn(acts[ch, 2].reshape(HALF, HID), wu)
        ).astype(BF16)

    def add(*parts):
        tot = parts[0].astype(F32)
        for p in parts[1:]:
            tot = tot + p.astype(F32)
        return tot

    def x_back_start(q):
        far = [
            send(e4.at[q, 2, x_lo], x_far.at[q, x_lo], at_x(1)), send(e4.at[q, 2, x_hi], x_far.at[q, x_hi], at_x(3))
        ]
        return far, [
            send(e4.at[q, 3, x_hi], x_in.at[q, 1, x_hi], at_x(1)), send(e4.at[q, 1, x_lo], x_in.at[q, 0, x_lo], at_x(3))
        ]

    def x_back_relay(q, started):
        far, rest = started
        far[0].wait_recv()
        e4[q, 3, x_lo] = add(e4[q, 3, x_lo], x_far[q, x_lo]).astype(BF16)
        rest.append(send(e4.at[q, 3, x_lo], x_in.at[q, 1, x_lo], at_x(1)))
        far[1].wait_recv()
        e4[q, 1, x_hi] = add(e4[q, 1, x_hi], x_far[q, x_hi]).astype(BF16)
        rest.append(send(e4.at[q, 1, x_hi], x_in.at[q, 0, x_hi], at_x(3)))
        return rest

    def y_back_start(buf, far, half, inn, cut):
        n = buf.shape[1]
        lo, hi = pl.ds(0, cut), pl.ds(cut, n - cut)
        first = [
            send(buf.at[4, lo], half.at[lo], at_y(6)), send(buf.at[3], far.at[0], at_y(7)),
            send(buf.at[4, hi], half.at[hi], at_y(2)), send(buf.at[5], far.at[1], at_y(1)),
        ]
        return first, [send(buf.at[1], inn.at[0], at_y(7)), send(buf.at[7], inn.at[1], at_y(1))]

    def y_back_relay(buf, far, half, inn, cut, started):
        n = buf.shape[1]
        lo, hi = pl.ds(0, cut), pl.ds(cut, n - cut)
        first, rest = started
        wait_all(first[:2])
        buf[2, lo] = add(buf[2, lo], far[0, lo], half[lo]).astype(BF16)
        buf[2, hi] = add(buf[2, hi], far[0, hi]).astype(BF16)
        rest.append(send(buf.at[2], inn.at[2], at_y(6)))
        wait_all(first[2:])
        buf[6, lo] = add(buf[6, lo], far[1, lo]).astype(BF16)
        buf[6, hi] = add(buf[6, hi], far[1, hi], half[hi]).astype(BF16)
        rest.append(send(buf.at[6], inn.at[3], at_y(2)))
        return rest

    def y_total(buf, inn):
        return add(buf[0], inn[0], inn[1], inn[2], inn[3])

    def unpack(table, tot):
        return dot_tn(table[...], tot.astype(BF16)).astype(BF16)

    small_back = [(u8.at[q], y_far8.at[q], y_half8.at[q], y_in8.at[q], BLK // 2) for q in range(3)]
    big_back = (e8, y_far_big, y_half_big, y_in_big, RB_CUT)

    def x_spread(q, rest):
        wait_all(rest)
        u8[q] = unpack(ta_ref, add(e4[q, 0], x_in[q, 0], x_in[q, 1])).reshape(NY, BLK, WID)
        return y_back_start(*small_back[q])

    def over_z(arr, tot):
        zo[arr] = tot.astype(BF16)
        return send(zo.at[arr], zo_in.at[arr], z_peer)

    def final_rows(arr):
        wait_all(ys[arr])
        tot = y_total(u8.at[arr], y_in8.at[arr])
        cz[arr].wait_recv()
        return dot_tn(sel, add(tot, zo_in[arr]).astype(BF16))

    def weight_grad(k, own, other):
        return dot_tn(acts[0, k].reshape(HALF, HID), rows_of(own)) + dot_tn(
            acts[1, k].reshape(HALF, HID), rows_of(other)
        )

    fa = to_core(0, fa)
    e4[0] = result(0, 0, fa).reshape(NX, RA, WID)
    xs[0] = x_back_start(0)
    fb = to_core(1, fb)
    e8[...] = result(1, 0, fb).reshape(NY, RB, WID)
    y_big = y_back_start(*big_back)
    bb = to_core(1, bb)
    e4[2] = dot_tn(perm_ref[...], result(1, 1, bb)).astype(BF16).reshape(NX, RA, WID)
    xs[2] = x_back_start(2)
    ba = to_core(0, ba)
    e4[1] = result(0, 1, ba).reshape(NX, RA, WID)
    xs[1] = x_back_start(1)
    xs[0] = x_back_relay(0, xs[0])
    y_big = y_back_relay(*big_back, y_big)
    xs[2] = x_back_relay(2, xs[2])
    ys[0] = x_spread(0, xs[0])
    xs[1] = x_back_relay(1, xs[1])
    dwg_ref[...] = weight_grad(1, "own tokens", "other tokens")
    keep(dwg_ref, dwg_hbm)
    ys[2] = x_spread(2, xs[2])
    wait_all(y_big)
    u4[...] = unpack(tb_ref, y_total(e8, y_in_big)).reshape(NX, BLK, WID)
    cx = [send(u4.at[k], u4_in.at[k - 1], at_x(NX - k)) for k in far_first_x]
    ys[1] = x_spread(1, xs[1])
    ys[0] = y_back_relay(*small_back[0], ys[0])
    ys[2] = y_back_relay(*small_back[2], ys[2])
    cz = [None, None]
    wait_all(cx)
    cz[0] = over_z(0, add(u4[0], u4_in[0], u4_in[1], u4_in[2]))
    ys[1] = y_back_relay(*small_back[1], ys[1])
    dwu_ref[...] = weight_grad(2, "own tokens", "other tokens")
    keep(dwu_ref, dwu_hbm)
    wait_all(ys[2])
    cz[1] = over_z(1, y_total(u8.at[2], y_in8.at[2]))
    dwd_ref[...] = weight_grad(0, "own grads", "other grads")
    keep(dwd_ref, dwd_hbm)
    out_rows = final_rows(0)
    gate_term = jnp.sum(cot_ref[...].astype(F32) * out_rows, axis=1, keepdims=True)
    row = jnp.sum(gate_term * eye, axis=0, keepdims=True)
    gsum[g] = jnp.broadcast_to(row, (8, TOK))
    cg = [send(gsum.at[g], gsum.at[g], at_group(j)) for j in (4, 3, 5, 2, 6, 1, 7)]
    token_gate = jnp.sum(eye * gate_row, axis=1, keepdims=True)
    mixed_ref[...] = (token_gate * out_rows).astype(BF16)
    keep(mixed_ref, mixed_hbm)
    tgrad_ref[...] = final_rows(1).astype(BF16)
    keep(tgrad_ref, tgrad_hbm)
    wait_all(cg)
    tot = gsum[0]
    for j in range(1, 8):
        tot = tot + gsum[j]
    ggrad_ref[...] = chosen * tot[0:1]
    keep(ggrad_ref, ggrad_hbm)
    for c in copies:
        c.wait_send()
    for c in stores:
        c.wait()


def store(*refs):
    ins, outs, mids, in_sems, out_sems = refs[:6], refs[6:12], refs[12:18], refs[18], refs[19]
    loads = [pltpu.make_async_copy(a, m, in_sems.at[i]) for i, (a, m) in enumerate(zip(ins, mids))]
    saves = [pltpu.make_async_copy(m, b, out_sems.at[i]) for i, (m, b) in enumerate(zip(mids, outs))]
    for c in loads:
        c.start()
    for load, save in zip(loads, saves):
        load.wait()
        save.start()
    for c in saves:
        c.wait()


def on_device(tokens, expert_ids, gates, gate_weight, up_weight, down_weight, cotangent):
    def vm(*shape, kind=BF16):
        return pltpu.VMEM(shape, kind)

    scratch = [
        vm(TOK, WID), vm(TOK, WID), vm(2, TOK, kind=F32),
        vm(HID, WID, kind=F32), vm(HID, WID, kind=F32), vm(HID, WID, kind=F32),
        vm(2, TOK, kind=jnp.int32), vm(2, TOK, kind=F32), vm(TOK, WID), vm(TOK, WID),
        vm(HID, WID), vm(HID, WID), vm(HID, WID),
        vm(3, NY, BLK, WID), vm(NX, BLK, WID), vm(3, NX, RA, WID), vm(NY, RB, WID), vm(HALF, WID),
        vm(2, 3, 8, OWN, HID), vm(2, 3, NZL, OWN, HID), vm(2, 3, NZL, OWN, HID),
        vm(2, 3, 3, OWN, HID), vm(2, 3, 8, OWN, HID),
        vm(3, NX, RA, WID), vm(3, 2, RA, WID), vm(3, RA, WID),
        vm(NY, RB, WID), vm(4, RB, WID), vm(2, RB, WID), vm(RB, WID),
        vm(3, NY, BLK, WID), vm(3, 4, BLK, WID), vm(3, 2, BLK, WID), vm(3, BLK, WID),
        vm(NX, BLK, WID), vm(NX - 1, BLK, WID),
        vm(2, BLK, WID), vm(2, BLK, WID), vm(8, 8, TOK, kind=F32),
        vm(RA, NY * BLK), vm(RB, NX * BLK), vm(HALF, HALF),
        pltpu.SemaphoreType.DMA((13,)),
        pltpu.SemaphoreType.DMA((N_COPIES,)), pltpu.SemaphoreType.DMA((N_COPIES,)),
    ]
    half = jax.ShapeDtypeStruct((TOK, WID), BF16)
    full = jax.ShapeDtypeStruct((TOK, WID), F32)
    shapes = (half, half, jax.ShapeDtypeStruct((2, TOK), F32), full, full, full)
    results = pl.pallas_call(
        kernel,
        out_shape=shapes,
        in_specs=[pl.BlockSpec(memory_space=pl.ANY)] * 7,
        out_specs=[pl.BlockSpec(memory_space=pl.ANY)] * 6,
        scratch_shapes=scratch,
        compiler_params=pltpu.CompilerParams(
            collective_id=0, has_side_effects=True, vmem_limit_bytes=VMEM_BYTES
        ),
    )(expert_ids.T, gates.T, tokens, cotangent, gate_weight, up_weight, down_weight)
    mixed, tgrad, ggrad, dwg, dwu, dwd = pl.pallas_call(
        store,
        out_shape=shapes,
        in_specs=[pl.BlockSpec(memory_space=pl.ANY)] * 6,
        out_specs=[pl.BlockSpec(memory_space=pl.ANY)] * 6,
        scratch_shapes=scratch[:6] + [pltpu.SemaphoreType.DMA((6,))] * 2,
        compiler_params=pltpu.CompilerParams(vmem_limit_bytes=VMEM_BYTES),
    )(*results)
    return mixed, tgrad, ggrad.T, dwg, dwu, dwd


def solution(mesh):
    wide, narrow = P("dp", "group"), P("dp", None)
    return jax.shard_map(
        on_device,
        mesh=mesh,
        in_specs=(wide, narrow, narrow, wide, wide, wide, wide),
        out_specs=(wide, wide, narrow, wide, wide, wide),
        check_vma=False,
    )
```

```python
import jax
import jax.numpy as jnp
from jax import lax
from jax.experimental import pallas as pl
from jax.experimental.pallas import tpu as pltpu
from jax.sharding import PartitionSpec as P

MESH = pl.DeviceIdType.MESH
F32 = jnp.float32
BF16 = jnp.bfloat16
CAP = 20
BLK = 32
NX, NY, NZL = 4, 8, 4
TOK, WID, HID = 128, 384, 128
RA = NY * CAP
RB = NX * CAP
HALF = NX * NY * CAP
OWN = HALF // 8
RB_CUT = 48
N_COPIES = 192
VMEM_BYTES = 64 * 1024 * 1024 - 64 * 1024


def dot_nt(a, b):
    return lax.dot_general(a, b, (((1,), (1,)), ((), ())), preferred_element_type=F32)


def dot_tn(a, b):
    return lax.dot_general(a, b, (((0,), (0,)), ((), ())), preferred_element_type=F32)


def dot_nn(a, b):
    return jnp.dot(a, b, preferred_element_type=F32)


def pack_table(blocks):
    rows, cols = blocks * CAP, blocks * BLK
    r = lax.broadcasted_iota(jnp.int32, (rows, cols), 0)
    c = lax.broadcasted_iota(jnp.int32, (rows, cols), 1)
    src = r
    for k in range(1, blocks):
        src = src + jnp.where(r >= k * CAP, BLK - CAP, 0)
    return (src == c).astype(F32).astype(BF16)


def order_table():
    r = lax.broadcasted_iota(jnp.int32, (HALF, TOK), 0)
    y = jnp.zeros_like(r)
    for k in range(1, NY):
        y = y + (r >= k * RB).astype(jnp.int32)
    x, q = jnp.zeros_like(r), r - y * RB
    for k in range(1, NX):
        x = x + (q >= k * CAP).astype(jnp.int32)
    src = x * RA + y * CAP + q - x * CAP
    c = lax.broadcasted_iota(jnp.int32, (HALF, TOK), 1)
    return jnp.concatenate(
        [(src == c + k * TOK).astype(F32).astype(BF16) for k in range(HALF // TOK)], axis=1
    )


def kernel(
    ids_hbm, gates_hbm, tok_hbm, cot_hbm, wg_hbm, wu_hbm, wd_hbm,
    mixed_hbm, tgrad_hbm, ggrad_hbm, dwg_hbm, dwu_hbm, dwd_hbm,
    mixed_ref, tgrad_ref, ggrad_ref, dwg_ref, dwu_ref, dwd_ref,
    ids_ref, gates_ref, tok_ref, cot_ref, wg_ref, wu_ref, wd_ref,
    g8, g4, big4, big8, ordered, part, core_in, core_sum, z_in, acts,
    e4, x_in, x_far, e8, y_in_big, y_far_big, y_half_big, u8, y_in8, y_far8, y_half8, u4, u4_in,
    dw_out, dw_in, gsum, ta_ref, tb_ref, perm_ref,
    local_sems, send_sems, recv_sems,
):
    d = lax.axis_index("dp")
    g = lax.axis_index("group")
    x = lax.rem(d, NX)
    y = lax.rem(lax.div(d, NX), NY)
    z = lax.div(d, NX * NY)
    core = lax.rem(g, 2)
    zl = lax.div(g, 2)

    def at_x(j):
        return {"dp": z * (NX * NY) + y * NX + lax.rem(x + j, NX)}

    def at_y(j):
        return {"dp": z * (NX * NY) + lax.rem(y + j, NY) * NX + x}

    z_peer = {"dp": (1 - z) * (NX * NY) + y * NX + x}
    core_peer = {"group": zl * 2 + (1 - core)}

    def at_zl(j):
        return {"group": lax.rem(zl + j, NZL) * 2 + core}

    def at_group(j):
        return {"group": lax.rem(g + j, 8)}

    copies = []

    def send(src, dst, device):
        k = len(copies)
        c = pltpu.make_async_remote_copy(
            src_ref=src, dst_ref=dst, send_sem=send_sems.at[k], recv_sem=recv_sems.at[k],
            device_id=device, device_id_type=MESH,
        )
        c.start()
        copies.append(c)
        return c

    def wait_all(cs):
        for c in cs:
            c.wait_recv()

    stores = []

    def keep(src, dst):
        c = pltpu.make_async_copy(src, dst, local_sems.at[7 + len(stores)])
        c.start()
        stores.append(c)

    barrier = pltpu.get_barrier_semaphore()
    partners = [z_peer] + [at_x(j) for j in range(1, NX)] + [at_y(j) for j in range(1, NY)]
    partners += [at_group(j) for j in range(1, 8)]
    for p in partners:
        pl.semaphore_signal(barrier, inc=1, device_id=p, device_id_type=MESH)
    pairs = (
        (ids_hbm, ids_ref), (gates_hbm, gates_ref), (tok_hbm, tok_ref), (cot_hbm, cot_ref),
        (wg_hbm, wg_ref.at[0]), (wu_hbm, wu_ref.at[0]), (wd_hbm, wd_ref.at[0]),
    )
    loads = []
    for i, (src, dst) in enumerate(pairs):
        c = pltpu.make_async_copy(src, dst, local_sems.at[i])
        c.start()
        loads.append(c)
    for c in loads[:4]:
        c.wait()

    chosen = (ids_ref[...] == 0).astype(F32)
    gate_row = jnp.sum(chosen * gates_ref[...], axis=0, keepdims=True)
    picked = jnp.broadcast_to(jnp.max(chosen, axis=0, keepdims=True), (BLK, TOK))
    ri = lax.broadcasted_iota(jnp.int32, (TOK, TOK), 0)
    ci = lax.broadcasted_iota(jnp.int32, (TOK, TOK), 1)
    eye = (ci == ri).astype(F32)
    before = dot_nn(picked.astype(BF16), (ri < ci).astype(F32).astype(BF16))
    slot = lax.broadcasted_iota(jnp.int32, (BLK, TOK), 0)
    hit = jnp.where((before == slot.astype(F32)) & (slot < CAP), picked, 0.0)
    sel = hit.astype(BF16)
    slot_gate = jnp.sum(hit * gate_row, axis=1, keepdims=True)
    g4[0] = dot_nn(sel, tok_ref[...]).astype(BF16)
    g8[0] = (slot_gate * dot_nn(sel, cot_ref[...])).astype(BF16)

    pl.semaphore_wait(barrier, len(partners))

    def y_start(buf):
        two = [send(buf.at[0], buf.at[j], at_y(j)) for j in (2, 6)]
        return two, [send(buf.at[0], buf.at[j], at_y(j)) for j in (1, 7)]

    def y_relay(buf, cut, started):
        two, rest = started
        n = buf.shape[1]
        lo, hi = pl.ds(0, cut), pl.ds(cut, n - cut)
        two[0].wait_recv()
        rest.append(send(buf.at[2, lo], buf.at[4, lo], at_y(2)))
        rest.append(send(buf.at[2], buf.at[3], at_y(1)))
        two[1].wait_recv()
        rest.append(send(buf.at[6, hi], buf.at[4, hi], at_y(6)))
        rest.append(send(buf.at[6], buf.at[5], at_y(7)))
        return rest

    x_lo, x_hi = pl.ds(0, RA // 2), pl.ds(RA // 2, RA // 2)

    def x_start(buf):
        first = [send(buf.at[0, x_lo], buf.at[1, x_lo], at_x(1)), send(buf.at[0, x_hi], buf.at[3, x_hi], at_x(3))]
        return first, [
            send(buf.at[0, x_hi], buf.at[1, x_hi], at_x(1)), send(buf.at[0, x_lo], buf.at[3, x_lo], at_x(3))
        ]

    def x_relay(buf, started):
        first, rest = started
        first[0].wait_recv()
        rest.append(send(buf.at[1, x_lo], buf.at[2, x_lo], at_x(1)))
        first[1].wait_recv()
        rest.append(send(buf.at[3, x_hi], buf.at[2, x_hi], at_x(3)))
        return rest

    def pack(table, blocks):
        n, _, _ = blocks.shape
        return dot_nn(table[...], blocks.reshape(n * BLK, WID)).astype(BF16)

    far_first_x = (2, 1, 3)
    cx = [send(g4.at[0], g4.at[j], at_x(j)) for j in far_first_x]
    ys = y_start(g8)
    for c in loads[4:]:
        c.wait()
    cz = [send(w.at[0], w.at[1], z_peer) for w in (wg_ref, wu_ref, wd_ref)]
    tb_ref[...] = pack_table(NX)
    ta_ref[...] = pack_table(NY)
    perm_ref[...] = order_table()
    wait_all(cx)
    big8[0] = pack(tb_ref, g4[...])
    y_big = y_start(big8)
    ys = y_relay(g8, BLK // 2, ys)
    wait_all(ys)
    big4[0] = pack(ta_ref, g8[...])
    x_big = x_start(big4)
    y_big = y_relay(big8, RB_CUT, y_big)
    x_big = x_relay(big4, x_big)
    wait_all(cz)

    def partials(ch, arr, rows):
        if arr == 0:
            part[ch, 0] = dot_nt(rows, wg_ref[ch]).astype(BF16).reshape(8, OWN, HID)
            part[ch, 1] = dot_nt(rows, wu_ref[ch]).astype(BF16).reshape(8, OWN, HID)
        else:
            part[ch, 2] = dot_nt(rows, wd_ref[ch]).astype(BF16).reshape(8, OWN, HID)
        ks = pl.ds(0, 2) if arr == 0 else pl.ds(2, 1)
        return send(part.at[ch, ks, pl.ds((1 - core) * NZL, NZL)], core_in.at[ch, ks], core_peer)

    def core_reduce(ch, arr, c):
        c.wait_recv()
        ks = pl.ds(0, 2) if arr == 0 else pl.ds(2, 1)
        mine = part[ch, ks, pl.ds(core * NZL, NZL)]
        core_sum[ch, ks] = (mine.astype(F32) + core_in[ch, ks].astype(F32)).astype(BF16)
        return [
            send(core_sum.at[ch, ks, lax.rem(zl + j, NZL)], z_in.at[ch, ks, j - 1], at_zl(j))
            for j in (3, 1, 2)
        ]

    def totals(ch, k):
        tot = core_sum[ch, k, zl].astype(F32)
        for j in range(3):
            tot = tot + z_in[ch, k, j].astype(F32)
        return tot

    own_row = core * NZL + zl

    def share(ch, ks):
        mine = acts.at[ch, ks, own_row]
        cs = {j: send(mine, mine, at_zl(j)) for j in (3, 1, 2)}
        return cs, [send(mine, mine, core_peer)], ks

    def act_forward(ch, cs):
        wait_all(cs)
        gate_act, up_act = totals(ch, 0), totals(ch, 1)
        sig = jax.nn.sigmoid(gate_act)
        silu = gate_act * sig
        acts[ch, 0, own_row] = (silu * up_act).astype(BF16)
        return share(ch, pl.ds(0, 1)), (silu, up_act * (sig * (1.0 + gate_act * (1.0 - sig))))

    def act_backward(ch, cs, kept):
        wait_all(cs)
        hidden_grad = totals(ch, 2)
        acts[ch, 1, own_row] = (hidden_grad * kept[1]).astype(BF16)
        acts[ch, 2, own_row] = (hidden_grad * kept[0]).astype(BF16)
        return share(ch, pl.ds(1, 2))

    def to_core(ch, shared):
        cs, near, ks = shared
        for j in (1, 3, 2):
            cs[j].wait_recv()
            theirs = acts.at[ch, ks, core * NZL + lax.rem(zl + NZL - j, NZL)]
            near.append(send(theirs, theirs, core_peer))
        return near

    def tok_rows():
        return big8[...].reshape(HALF, WID)

    wait_all(y_big)
    core_t = [partials(h, 0, tok_rows()) for h in range(2)]
    zt = [core_reduce(h, 0, core_t[h]) for h in range(2)]
    wait_all(x_big)
    ordered[...] = dot_nn(perm_ref[...], big4[...].reshape(HALF, WID)).astype(BF16)
    core_g = [partials(h, 1, ordered[...]) for h in range(2)]
    zg = [core_reduce(h, 1, core_g[h]) for h in range(2)]
    f0, kept_0 = act_forward(0, zt[0])
    f1, kept_1 = act_forward(1, zt[1])
    b0 = act_backward(0, zg[0], kept_0)
    b1 = act_backward(1, zg[1], kept_1)

    def product(k, w_ref):
        return dot_nn(acts[0, k].reshape(HALF, HID), w_ref[0]) + dot_nn(acts[1, k].reshape(HALF, HID), w_ref[1])

    def add(*parts):
        tot = parts[0].astype(F32)
        for p in parts[1:]:
            tot = tot + p.astype(F32)
        return tot

    def x_back_start():
        far = [
            send(e4.at[2, x_lo], x_far.at[x_lo], at_x(1)), send(e4.at[2, x_hi], x_far.at[x_hi], at_x(3))
        ]
        return far, [
            send(e4.at[3, x_hi], x_in.at[1, x_hi], at_x(1)), send(e4.at[1, x_lo], x_in.at[0, x_lo], at_x(3))
        ]

    def x_back_relay(started):
        far, rest = started
        far[0].wait_recv()
        e4[3, x_lo] = add(e4[3, x_lo], x_far[x_lo]).astype(BF16)
        rest.append(send(e4.at[3, x_lo], x_in.at[1, x_lo], at_x(1)))
        far[1].wait_recv()
        e4[1, x_hi] = add(e4[1, x_hi], x_far[x_hi]).astype(BF16)
        rest.append(send(e4.at[1, x_hi], x_in.at[0, x_hi], at_x(3)))
        return rest

    def y_back_start(buf, far, half, inn, cut):
        n = buf.shape[1]
        lo, hi = pl.ds(0, cut), pl.ds(cut, n - cut)
        first = [
            send(buf.at[4, lo], half.at[lo], at_y(6)), send(buf.at[3], far.at[0], at_y(7)),
            send(buf.at[4, hi], half.at[hi], at_y(2)), send(buf.at[5], far.at[1], at_y(1)),
        ]
        return first, [send(buf.at[1], inn.at[0], at_y(7)), send(buf.at[7], inn.at[1], at_y(1))]

    def y_back_relay(buf, far, half, inn, cut, started):
        n = buf.shape[1]
        lo, hi = pl.ds(0, cut), pl.ds(cut, n - cut)
        first, rest = started
        wait_all(first[:2])
        buf[2, lo] = add(buf[2, lo], far[0, lo], half[lo]).astype(BF16)
        buf[2, hi] = add(buf[2, hi], far[0, hi]).astype(BF16)
        rest.append(send(buf.at[2], inn.at[2], at_y(6)))
        wait_all(first[2:])
        buf[6, lo] = add(buf[6, lo], far[1, lo]).astype(BF16)
        buf[6, hi] = add(buf[6, hi], far[1, hi], half[hi]).astype(BF16)
        rest.append(send(buf.at[6], inn.at[3], at_y(2)))
        return rest

    def y_total(buf, inn):
        return add(buf[0], inn[0], inn[1], inn[2], inn[3])

    def unpack(table, tot):
        return dot_tn(table[...], tot.astype(BF16)).astype(BF16)

    small_back = (u8, y_far8, y_half8, y_in8, BLK // 2)
    big_back = (e8, y_far_big, y_half_big, y_in_big, RB_CUT)

    def weight_grad(h, k, rows):
        return dot_tn(acts[h, k].reshape(HALF, HID), rows)

    def grad_rows(k):
        return ordered[...] if k == 0 else tok_rows()

    near0, near1 = to_core(0, f0), to_core(1, f1)
    wait_all(near0 + near1)
    e8[...] = product(0, wd_ref).astype(BF16).reshape(NY, RB, WID)
    y_big = y_back_start(*big_back)
    near0, near1 = to_core(0, b0), to_core(1, b1)
    wait_all(near0 + near1)
    e4[...] = dot_tn(perm_ref[...], (product(1, wg_ref) + product(2, wu_ref)).astype(BF16)).astype(BF16).reshape(
        NX, RA, WID
    )
    x_big = x_back_start()
    cz = {}

    def swap_grad(k):
        dw_out[k] = weight_grad(1, k, grad_rows(k)).astype(BF16)
        cz[k] = send(dw_out.at[k], dw_in.at[k], z_peer)

    swap_grad(1)
    y_big = y_back_relay(*big_back, y_big)
    swap_grad(2)
    x_big = x_back_relay(x_big)
    swap_grad(0)
    wait_all(x_big)
    u8[...] = unpack(ta_ref, add(e4[0], x_in[0], x_in[1])).reshape(NY, BLK, WID)
    ys = y_back_start(*small_back)
    wait_all(y_big)
    u4[...] = unpack(tb_ref, y_total(e8, y_in_big)).reshape(NX, BLK, WID)
    cx = [send(u4.at[k], u4_in.at[k - 1], at_x(NX - k)) for k in far_first_x]
    outs = {1: (dwg_ref, dwg_hbm), 2: (dwu_ref, dwu_hbm), 0: (dwd_ref, dwd_hbm)}
    for k in (1, 2, 0):
        outs[k][0][...] = weight_grad(0, k, grad_rows(k))
    ys = y_back_relay(*small_back, ys)
    wait_all(cx)
    out_rows = dot_tn(sel, add(u4[0], u4_in[0], u4_in[1], u4_in[2]).astype(BF16))
    gate_term = jnp.sum(cot_ref[...].astype(F32) * out_rows, axis=1, keepdims=True)
    row = jnp.sum(gate_term * eye, axis=0, keepdims=True)
    gsum[g] = jnp.broadcast_to(row, (8, TOK))
    cg = [send(gsum.at[g], gsum.at[g], at_group(j)) for j in (4, 3, 5, 2, 6, 1, 7)]
    token_gate = jnp.sum(eye * gate_row, axis=1, keepdims=True)
    mixed_ref[...] = (token_gate * out_rows).astype(BF16)
    keep(mixed_ref, mixed_hbm)
    for k in (1, 2, 0):
        cz[k].wait_recv()
        outs[k][0][...] += dw_in[k].astype(F32)
        keep(*outs[k])
    wait_all(ys)
    tgrad_ref[...] = dot_tn(sel, y_total(u8, y_in8).astype(BF16)).astype(BF16)
    keep(tgrad_ref, tgrad_hbm)
    wait_all(cg)
    tot = gsum[0]
    for j in range(1, 8):
        tot = tot + gsum[j]
    ggrad_ref[...] = chosen * tot[0:1]
    keep(ggrad_ref, ggrad_hbm)
    for c in copies:
        c.wait_send()
    for c in stores:
        c.wait()


def store(*refs):
    ins, outs, mids, in_sems, out_sems = refs[:6], refs[6:12], refs[12:18], refs[18], refs[19]
    loads = [pltpu.make_async_copy(a, m, in_sems.at[i]) for i, (a, m) in enumerate(zip(ins, mids))]
    saves = [pltpu.make_async_copy(m, b, out_sems.at[i]) for i, (m, b) in enumerate(zip(mids, outs))]
    for c in loads:
        c.start()
    for load, save in zip(loads, saves):
        load.wait()
        save.start()
    for c in saves:
        c.wait()


def on_device(tokens, expert_ids, gates, gate_weight, up_weight, down_weight, cotangent):
    def vm(*shape, kind=BF16):
        return pltpu.VMEM(shape, kind)

    scratch = [
        vm(TOK, WID), vm(TOK, WID), vm(2, TOK, kind=F32),
        vm(HID, WID, kind=F32), vm(HID, WID, kind=F32), vm(HID, WID, kind=F32),
        vm(2, TOK, kind=jnp.int32), vm(2, TOK, kind=F32), vm(TOK, WID), vm(TOK, WID),
        vm(2, HID, WID), vm(2, HID, WID), vm(2, HID, WID),
        vm(NY, BLK, WID), vm(NX, BLK, WID), vm(NX, RA, WID), vm(NY, RB, WID), vm(HALF, WID),
        vm(2, 3, 8, OWN, HID), vm(2, 3, NZL, OWN, HID), vm(2, 3, NZL, OWN, HID),
        vm(2, 3, 3, OWN, HID), vm(2, 3, 8, OWN, HID),
        vm(NX, RA, WID), vm(2, RA, WID), vm(RA, WID),
        vm(NY, RB, WID), vm(4, RB, WID), vm(2, RB, WID), vm(RB, WID),
        vm(NY, BLK, WID), vm(4, BLK, WID), vm(2, BLK, WID), vm(BLK, WID),
        vm(NX, BLK, WID), vm(NX - 1, BLK, WID),
        vm(3, HID, WID), vm(3, HID, WID), vm(8, 8, TOK, kind=F32),
        vm(RA, NY * BLK), vm(RB, NX * BLK), vm(HALF, HALF),
        pltpu.SemaphoreType.DMA((13,)),
        pltpu.SemaphoreType.DMA((N_COPIES,)), pltpu.SemaphoreType.DMA((N_COPIES,)),
    ]
    half = jax.ShapeDtypeStruct((TOK, WID), BF16)
    full = jax.ShapeDtypeStruct((TOK, WID), F32)
    shapes = (half, half, jax.ShapeDtypeStruct((2, TOK), F32), full, full, full)
    results = pl.pallas_call(
        kernel,
        out_shape=shapes,
        in_specs=[pl.BlockSpec(memory_space=pl.ANY)] * 7,
        out_specs=[pl.BlockSpec(memory_space=pl.ANY)] * 6,
        scratch_shapes=scratch,
        compiler_params=pltpu.CompilerParams(
            collective_id=0, has_side_effects=True, vmem_limit_bytes=VMEM_BYTES
        ),
    )(expert_ids.T, gates.T, tokens, cotangent, gate_weight, up_weight, down_weight)
    mixed, tgrad, ggrad, dwg, dwu, dwd = pl.pallas_call(
        store,
        out_shape=shapes,
        in_specs=[pl.BlockSpec(memory_space=pl.ANY)] * 6,
        out_specs=[pl.BlockSpec(memory_space=pl.ANY)] * 6,
        scratch_shapes=scratch[:6] + [pltpu.SemaphoreType.DMA((6,))] * 2,
        compiler_params=pltpu.CompilerParams(vmem_limit_bytes=VMEM_BYTES),
    )(*results)
    return mixed, tgrad, ggrad.T, dwg, dwu, dwd


def solution(mesh):
    wide, narrow = P("dp", "group"), P("dp", None)
    return jax.shard_map(
        on_device,
        mesh=mesh,
        in_specs=(wide, narrow, narrow, wide, wide, wide, wide),
        out_specs=(wide, wide, narrow, wide, wide, wide),
        check_vma=False,
    )
```

```python
import jax
import jax.numpy as jnp
from jax import lax
from jax.experimental import pallas as pl
from jax.experimental.pallas import tpu as pltpu
from jax.sharding import PartitionSpec as P

MESH = pl.DeviceIdType.MESH
F32 = jnp.float32
BF16 = jnp.bfloat16
CAP = 20
BLK = 32
NX, NY, NZL = 4, 8, 4
TOK, WID, HID = 128, 384, 128
RB = NX * CAP
HALF = NX * NY * CAP
OWN = HALF // 8
RB_CUT = 48
N_COPIES = 192
VMEM_BYTES = 64 * 1024 * 1024 - 64 * 1024


def dot_nt(a, b):
    return lax.dot_general(a, b, (((1,), (1,)), ((), ())), preferred_element_type=F32)


def dot_tn(a, b):
    return lax.dot_general(a, b, (((0,), (0,)), ((), ())), preferred_element_type=F32)


def dot_nn(a, b):
    return jnp.dot(a, b, preferred_element_type=F32)


def pack_table(blocks):
    rows, cols = blocks * CAP, blocks * BLK
    r = lax.broadcasted_iota(jnp.int32, (rows, cols), 0)
    c = lax.broadcasted_iota(jnp.int32, (rows, cols), 1)
    src = r
    for k in range(1, blocks):
        src = src + jnp.where(r >= k * CAP, BLK - CAP, 0)
    return (src == c).astype(F32).astype(BF16)


def kernel(
    ids_hbm, gates_hbm, tok_hbm, cot_hbm, wg_hbm, wu_hbm, wd_hbm,
    mixed_hbm, tgrad_hbm, ggrad_hbm, dwg_hbm, dwu_hbm, dwd_hbm,
    mixed_ref, tgrad_ref, ggrad_ref, dwg_ref, dwu_ref, dwd_ref,
    ids_ref, gates_ref, tok_ref, cot_ref, wg_ref, wu_ref, wd_ref,
    g4, big8, part, core_in, core_sum, z_in, acts,
    e8, y_in, y_far, y_half, u4, u4_in, dw_out, dw_in, gsum, tb_ref,
    local_sems, send_sems, recv_sems,
):
    d = lax.axis_index("dp")
    g = lax.axis_index("group")
    x = lax.rem(d, NX)
    y = lax.rem(lax.div(d, NX), NY)
    z = lax.div(d, NX * NY)
    core = lax.rem(g, 2)
    zl = lax.div(g, 2)

    def at_x(j):
        return {"dp": z * (NX * NY) + y * NX + lax.rem(x + j, NX)}

    def at_y(j):
        return {"dp": z * (NX * NY) + lax.rem(y + j, NY) * NX + x}

    z_peer = {"dp": (1 - z) * (NX * NY) + y * NX + x}
    core_peer = {"group": zl * 2 + (1 - core)}

    def at_zl(j):
        return {"group": lax.rem(zl + j, NZL) * 2 + core}

    def at_group(j):
        return {"group": lax.rem(g + j, 8)}

    copies = []

    def send(src, dst, device):
        k = len(copies)
        c = pltpu.make_async_remote_copy(
            src_ref=src, dst_ref=dst, send_sem=send_sems.at[k], recv_sem=recv_sems.at[k],
            device_id=device, device_id_type=MESH,
        )
        c.start()
        copies.append(c)
        return c

    def wait_all(cs):
        for c in cs:
            c.wait_recv()

    stores = []

    def keep(src, dst):
        c = pltpu.make_async_copy(src, dst, local_sems.at[7 + len(stores)])
        c.start()
        stores.append(c)

    barrier = pltpu.get_barrier_semaphore()
    partners = [z_peer] + [at_x(j) for j in range(1, NX)] + [at_y(j) for j in range(1, NY)]
    partners += [at_group(j) for j in range(1, 8)]
    for p in partners:
        pl.semaphore_signal(barrier, inc=1, device_id=p, device_id_type=MESH)
    pairs = (
        (ids_hbm, ids_ref), (gates_hbm, gates_ref), (tok_hbm, tok_ref), (cot_hbm, cot_ref),
        (wg_hbm, wg_ref.at[0]), (wu_hbm, wu_ref.at[0]), (wd_hbm, wd_ref.at[0]),
    )
    loads = []
    for i, (src, dst) in enumerate(pairs):
        c = pltpu.make_async_copy(src, dst, local_sems.at[i])
        c.start()
        loads.append(c)
    for c in loads[:4]:
        c.wait()

    chosen = (ids_ref[...] == 0).astype(F32)
    gate_row = jnp.sum(chosen * gates_ref[...], axis=0, keepdims=True)
    picked = jnp.broadcast_to(jnp.max(chosen, axis=0, keepdims=True), (BLK, TOK))
    ri = lax.broadcasted_iota(jnp.int32, (TOK, TOK), 0)
    ci = lax.broadcasted_iota(jnp.int32, (TOK, TOK), 1)
    eye = (ci == ri).astype(F32)
    before = dot_nn(picked.astype(BF16), (ri < ci).astype(F32).astype(BF16))
    slot = lax.broadcasted_iota(jnp.int32, (BLK, TOK), 0)
    hit = jnp.where((before == slot.astype(F32)) & (slot < CAP), picked, 0.0)
    sel = hit.astype(BF16)
    slot_gate = jnp.sum(hit * gate_row, axis=1, keepdims=True)
    g4[0, 0] = dot_nn(sel, tok_ref[...]).astype(BF16)
    g4[1, 0] = (slot_gate * dot_nn(sel, cot_ref[...])).astype(BF16)

    pl.semaphore_wait(barrier, len(partners))

    def y_start(buf):
        two = [send(buf.at[0], buf.at[j], at_y(j)) for j in (2, 6)]
        return two, [send(buf.at[0], buf.at[j], at_y(j)) for j in (1, 7)]

    def y_relay(buf, cut, started):
        two, rest = started
        n = buf.shape[1]
        lo, hi = pl.ds(0, cut), pl.ds(cut, n - cut)
        two[0].wait_recv()
        rest.append(send(buf.at[2, lo], buf.at[4, lo], at_y(2)))
        rest.append(send(buf.at[2], buf.at[3], at_y(1)))
        two[1].wait_recv()
        rest.append(send(buf.at[6, hi], buf.at[4, hi], at_y(6)))
        rest.append(send(buf.at[6], buf.at[5], at_y(7)))
        return rest

    def pack(table, blocks):
        n, _, _ = blocks.shape
        return dot_nn(table[...], blocks.reshape(n * BLK, WID)).astype(BF16)

    far_first_x = (2, 1, 3)
    cx = [[send(g4.at[arr, 0], g4.at[arr, j], at_x(j)) for j in far_first_x] for arr in range(2)]
    for c in loads[4:]:
        c.wait()
    cz = [send(w.at[0], w.at[1], z_peer) for w in (wg_ref, wu_ref, wd_ref)]
    tb_ref[...] = pack_table(NX)
    ys = [None, None]
    for arr in range(2):
        wait_all(cx[arr])
        big8[arr, 0] = pack(tb_ref, g4[arr])
        ys[arr] = y_start(big8.at[arr])
    for arr in range(2):
        ys[arr] = y_relay(big8.at[arr], RB_CUT, ys[arr])
    wait_all(cz)

    def partials(ch, arr, rows):
        if arr == 0:
            part[ch, 0] = dot_nt(rows, wg_ref[ch]).astype(BF16).reshape(8, OWN, HID)
            part[ch, 1] = dot_nt(rows, wu_ref[ch]).astype(BF16).reshape(8, OWN, HID)
        else:
            part[ch, 2] = dot_nt(rows, wd_ref[ch]).astype(BF16).reshape(8, OWN, HID)
        ks = pl.ds(0, 2) if arr == 0 else pl.ds(2, 1)
        return send(part.at[ch, ks, pl.ds((1 - core) * NZL, NZL)], core_in.at[ch, ks], core_peer)

    def core_reduce(ch, arr, c):
        c.wait_recv()
        ks = pl.ds(0, 2) if arr == 0 else pl.ds(2, 1)
        mine = part[ch, ks, pl.ds(core * NZL, NZL)]
        core_sum[ch, ks] = (mine.astype(F32) + core_in[ch, ks].astype(F32)).astype(BF16)
        return [
            send(core_sum.at[ch, ks, lax.rem(zl + j, NZL)], z_in.at[ch, ks, j - 1], at_zl(j))
            for j in (3, 1, 2)
        ]

    def totals(ch, k):
        tot = core_sum[ch, k, zl].astype(F32)
        for j in range(3):
            tot = tot + z_in[ch, k, j].astype(F32)
        return tot

    own_row = core * NZL + zl

    def share(ch, ks):
        mine = acts.at[ch, ks, own_row]
        cs = {j: send(mine, mine, at_zl(j)) for j in (3, 1, 2)}
        return cs, [send(mine, mine, core_peer)], ks

    def act_forward(ch, cs):
        wait_all(cs)
        gate_act, up_act = totals(ch, 0), totals(ch, 1)
        sig = jax.nn.sigmoid(gate_act)
        silu = gate_act * sig
        acts[ch, 0, own_row] = (silu * up_act).astype(BF16)
        return share(ch, pl.ds(0, 1)), (silu, up_act * (sig * (1.0 + gate_act * (1.0 - sig))))

    def act_backward(ch, cs, kept):
        wait_all(cs)
        hidden_grad = totals(ch, 2)
        acts[ch, 1, own_row] = (hidden_grad * kept[1]).astype(BF16)
        acts[ch, 2, own_row] = (hidden_grad * kept[0]).astype(BF16)
        return share(ch, pl.ds(1, 2))

    def to_core(ch, shared):
        cs, near, ks = shared
        for j in (1, 3, 2):
            cs[j].wait_recv()
            theirs = acts.at[ch, ks, core * NZL + lax.rem(zl + NZL - j, NZL)]
            near.append(send(theirs, theirs, core_peer))
        return near

    def rows_of(arr):
        return big8[arr].reshape(HALF, WID)

    wait_all(ys[0])
    core_t = [partials(h, 0, rows_of(0)) for h in range(2)]
    zt = [core_reduce(h, 0, core_t[h]) for h in range(2)]
    wait_all(ys[1])
    core_g = [partials(h, 1, rows_of(1)) for h in range(2)]
    zg = [core_reduce(h, 1, core_g[h]) for h in range(2)]
    f0, kept_0 = act_forward(0, zt[0])
    f1, kept_1 = act_forward(1, zt[1])
    b0 = act_backward(0, zg[0], kept_0)
    b1 = act_backward(1, zg[1], kept_1)

    def product(k, w_ref):
        return dot_nn(acts[0, k].reshape(HALF, HID), w_ref[0]) + dot_nn(acts[1, k].reshape(HALF, HID), w_ref[1])

    def add(*parts):
        tot = parts[0].astype(F32)
        for p in parts[1:]:
            tot = tot + p.astype(F32)
        return tot

    def y_back_start(buf, far, half, inn, cut):
        n = buf.shape[1]
        lo, hi = pl.ds(0, cut), pl.ds(cut, n - cut)
        first = [
            send(buf.at[4, lo], half.at[lo], at_y(6)), send(buf.at[3], far.at[0], at_y(7)),
            send(buf.at[4, hi], half.at[hi], at_y(2)), send(buf.at[5], far.at[1], at_y(1)),
        ]
        return first, [send(buf.at[1], inn.at[0], at_y(7)), send(buf.at[7], inn.at[1], at_y(1))]

    def y_back_relay(buf, far, half, inn, cut, started):
        n = buf.shape[1]
        lo, hi = pl.ds(0, cut), pl.ds(cut, n - cut)
        first, rest = started
        wait_all(first[:2])
        buf[2, lo] = add(buf[2, lo], far[0, lo], half[lo]).astype(BF16)
        buf[2, hi] = add(buf[2, hi], far[0, hi]).astype(BF16)
        rest.append(send(buf.at[2], inn.at[2], at_y(6)))
        wait_all(first[2:])
        buf[6, lo] = add(buf[6, lo], far[1, lo]).astype(BF16)
        buf[6, hi] = add(buf[6, hi], far[1, hi], half[hi]).astype(BF16)
        rest.append(send(buf.at[6], inn.at[3], at_y(2)))
        return rest

    def y_total(buf, inn):
        return add(buf[0], inn[0], inn[1], inn[2], inn[3])

    def unpack(table, tot):
        return dot_tn(table[...], tot.astype(BF16)).astype(BF16)

    big_back = [(e8.at[q], y_far.at[q], y_half.at[q], y_in.at[q], RB_CUT) for q in range(2)]

    def weight_grad(h, k):
        return dot_tn(acts[h, k].reshape(HALF, HID), rows_of(1 if k == 0 else 0))

    near0, near1 = to_core(0, f0), to_core(1, f1)
    wait_all(near0 + near1)
    e8[0] = product(0, wd_ref).astype(BF16).reshape(NY, RB, WID)
    ys[0] = y_back_start(*big_back[0])
    near0, near1 = to_core(0, b0), to_core(1, b1)
    wait_all(near0 + near1)
    e8[1] = (product(1, wg_ref) + product(2, wu_ref)).astype(BF16).reshape(NY, RB, WID)
    ys[1] = y_back_start(*big_back[1])
    cz = {}

    def swap_grad(k):
        dw_out[k] = weight_grad(1, k).astype(BF16)
        cz[k] = send(dw_out.at[k], dw_in.at[k], z_peer)

    def x_spread(q):
        wait_all(ys[q])
        u4[q] = unpack(tb_ref, y_total(e8.at[q], y_in.at[q])).reshape(NX, BLK, WID)
        return [send(u4.at[q, k], u4_in.at[q, k - 1], at_x(NX - k)) for k in far_first_x]

    ys[0] = y_back_relay(*big_back[0], ys[0])
    swap_grad(1)
    swap_grad(2)
    ys[1] = y_back_relay(*big_back[1], ys[1])
    swap_grad(0)
    cx[0] = x_spread(0)
    outs = {1: (dwg_ref, dwg_hbm), 2: (dwu_ref, dwu_hbm), 0: (dwd_ref, dwd_hbm)}
    for k in (1, 2, 0):
        outs[k][0][...] = weight_grad(0, k)

    def final_rows(q):
        wait_all(cx[q])
        return dot_tn(sel, add(u4[q, 0], u4_in[q, 0], u4_in[q, 1], u4_in[q, 2]).astype(BF16))

    out_rows = final_rows(0)
    gate_term = jnp.sum(cot_ref[...].astype(F32) * out_rows, axis=1, keepdims=True)
    row = jnp.sum(gate_term * eye, axis=0, keepdims=True)
    gsum[g] = jnp.broadcast_to(row, (8, TOK))
    cg = [send(gsum.at[g], gsum.at[g], at_group(j)) for j in (4, 3, 5, 2, 6, 1, 7)]
    cx[1] = x_spread(1)
    token_gate = jnp.sum(eye * gate_row, axis=1, keepdims=True)
    mixed_ref[...] = (token_gate * out_rows).astype(BF16)
    keep(mixed_ref, mixed_hbm)
    for k in (1, 2, 0):
        cz[k].wait_recv()
        outs[k][0][...] += dw_in[k].astype(F32)
        keep(*outs[k])
    tgrad_ref[...] = final_rows(1).astype(BF16)
    keep(tgrad_ref, tgrad_hbm)
    wait_all(cg)
    tot = gsum[0]
    for j in range(1, 8):
        tot = tot + gsum[j]
    ggrad_ref[...] = chosen * tot[0:1]
    keep(ggrad_ref, ggrad_hbm)
    for c in copies:
        c.wait_send()
    for c in stores:
        c.wait()


def store(*refs):
    ins, outs, mids, in_sems, out_sems = refs[:6], refs[6:12], refs[12:18], refs[18], refs[19]
    loads = [pltpu.make_async_copy(a, m, in_sems.at[i]) for i, (a, m) in enumerate(zip(ins, mids))]
    saves = [pltpu.make_async_copy(m, b, out_sems.at[i]) for i, (m, b) in enumerate(zip(mids, outs))]
    for c in loads:
        c.start()
    for load, save in zip(loads, saves):
        load.wait()
        save.start()
    for c in saves:
        c.wait()


def on_device(tokens, expert_ids, gates, gate_weight, up_weight, down_weight, cotangent):
    def vm(*shape, kind=BF16):
        return pltpu.VMEM(shape, kind)

    scratch = [
        vm(TOK, WID), vm(TOK, WID), vm(2, TOK, kind=F32),
        vm(HID, WID, kind=F32), vm(HID, WID, kind=F32), vm(HID, WID, kind=F32),
        vm(2, TOK, kind=jnp.int32), vm(2, TOK, kind=F32), vm(TOK, WID), vm(TOK, WID),
        vm(2, HID, WID), vm(2, HID, WID), vm(2, HID, WID),
        vm(2, NX, BLK, WID), vm(2, NY, RB, WID),
        vm(2, 3, 8, OWN, HID), vm(2, 3, NZL, OWN, HID), vm(2, 3, NZL, OWN, HID),
        vm(2, 3, 3, OWN, HID), vm(2, 3, 8, OWN, HID),
        vm(2, NY, RB, WID), vm(2, 4, RB, WID), vm(2, 2, RB, WID), vm(2, RB, WID),
        vm(2, NX, BLK, WID), vm(2, NX - 1, BLK, WID),
        vm(3, HID, WID), vm(3, HID, WID), vm(8, 8, TOK, kind=F32),
        vm(RB, NX * BLK),
        pltpu.SemaphoreType.DMA((13,)),
        pltpu.SemaphoreType.DMA((N_COPIES,)), pltpu.SemaphoreType.DMA((N_COPIES,)),
    ]
    half = jax.ShapeDtypeStruct((TOK, WID), BF16)
    full = jax.ShapeDtypeStruct((TOK, WID), F32)
    shapes = (half, half, jax.ShapeDtypeStruct((2, TOK), F32), full, full, full)
    results = pl.pallas_call(
        kernel,
        out_shape=shapes,
        in_specs=[pl.BlockSpec(memory_space=pl.ANY)] * 7,
        out_specs=[pl.BlockSpec(memory_space=pl.ANY)] * 6,
        scratch_shapes=scratch,
        compiler_params=pltpu.CompilerParams(
            collective_id=0, has_side_effects=True, vmem_limit_bytes=VMEM_BYTES
        ),
    )(expert_ids.T, gates.T, tokens, cotangent, gate_weight, up_weight, down_weight)
    mixed, tgrad, ggrad, dwg, dwu, dwd = pl.pallas_call(
        store,
        out_shape=shapes,
        in_specs=[pl.BlockSpec(memory_space=pl.ANY)] * 6,
        out_specs=[pl.BlockSpec(memory_space=pl.ANY)] * 6,
        scratch_shapes=scratch[:6] + [pltpu.SemaphoreType.DMA((6,))] * 2,
        compiler_params=pltpu.CompilerParams(vmem_limit_bytes=VMEM_BYTES),
    )(*results)
    return mixed, tgrad, ggrad.T, dwg, dwu, dwd


def solution(mesh):
    wide, narrow = P("dp", "group"), P("dp", None)
    return jax.shard_map(
        on_device,
        mesh=mesh,
        in_specs=(wide, narrow, narrow, wide, wide, wide, wide),
        out_specs=(wide, wide, narrow, wide, wide, wide),
        check_vma=False,
    )
```

```python
import jax
import jax.numpy as jnp
from jax import lax
from jax.experimental import pallas as pl
from jax.experimental.pallas import tpu as pltpu
from jax.sharding import PartitionSpec as P

MESH = pl.DeviceIdType.MESH
F32 = jnp.float32
BF16 = jnp.bfloat16
CAP = 20
BLK = 32
NX, NY, NZL = 4, 8, 4
TOK, WID, HID = 128, 384, 128
RA = NY * CAP
RB = NX * CAP
HALF = NX * NY * CAP
OWN = HALF // 8
RB_CUT = 48
N_COPIES = 192
VMEM_BYTES = 64 * 1024 * 1024 - 64 * 1024


def dot_nt(a, b):
    return lax.dot_general(a, b, (((1,), (1,)), ((), ())), preferred_element_type=F32)


def dot_tn(a, b):
    return lax.dot_general(a, b, (((0,), (0,)), ((), ())), preferred_element_type=F32)


def dot_nn(a, b):
    return jnp.dot(a, b, preferred_element_type=F32)


def pack_table(blocks):
    rows, cols = blocks * CAP, blocks * BLK
    r = lax.broadcasted_iota(jnp.int32, (rows, cols), 0)
    c = lax.broadcasted_iota(jnp.int32, (rows, cols), 1)
    src = r
    for k in range(1, blocks):
        src = src + jnp.where(r >= k * CAP, BLK - CAP, 0)
    return (src == c).astype(F32).astype(BF16)


def order_table():
    r = lax.broadcasted_iota(jnp.int32, (HALF, TOK), 0)
    y = jnp.zeros_like(r)
    for k in range(1, NY):
        y = y + (r >= k * RB).astype(jnp.int32)
    x, q = jnp.zeros_like(r), r - y * RB
    for k in range(1, NX):
        x = x + (q >= k * CAP).astype(jnp.int32)
    src = x * RA + y * CAP + q - x * CAP
    c = lax.broadcasted_iota(jnp.int32, (HALF, TOK), 1)
    return jnp.concatenate(
        [(src == c + k * TOK).astype(F32).astype(BF16) for k in range(HALF // TOK)], axis=1
    )


def kernel(
    ids_hbm, gates_hbm, tok_hbm, cot_hbm, wg_hbm, wu_hbm, wd_hbm,
    mixed_hbm, tgrad_hbm, ggrad_hbm, dwg_hbm, dwu_hbm, dwd_hbm,
    mixed_ref, tgrad_ref, ggrad_ref, dwg_ref, dwu_ref, dwd_ref,
    ids_ref, gates_ref, tok_ref, cot_ref, wg_ref, wu_ref, wd_ref,
    g8, g4, big4, big8, ordered, part, core_in, core_sum, z_in, acts,
    e4, x_in, x_far, e8, y_in_big, y_far_big, y_half_big, u8, y_in8, y_far8, y_half8, u4, u4_in,
    dw_out, dw_in, gsum, ta_ref, tb_ref, perm_ref,
    local_sems, send_sems, recv_sems,
):
    d = lax.axis_index("dp")
    g = lax.axis_index("group")
    x = lax.rem(d, NX)
    y = lax.rem(lax.div(d, NX), NY)
    z = lax.div(d, NX * NY)
    core = lax.rem(g, 2)
    zl = lax.div(g, 2)

    def at_x(j):
        return {"dp": z * (NX * NY) + y * NX + lax.rem(x + j, NX)}

    def at_y(j):
        return {"dp": z * (NX * NY) + lax.rem(y + j, NY) * NX + x}

    z_peer = {"dp": (1 - z) * (NX * NY) + y * NX + x}
    core_peer = {"group": zl * 2 + (1 - core)}

    def at_zl(j):
        return {"group": lax.rem(zl + j, NZL) * 2 + core}

    def at_group(j):
        return {"group": lax.rem(g + j, 8)}

    copies = []

    def send(src, dst, device):
        k = len(copies)
        c = pltpu.make_async_remote_copy(
            src_ref=src, dst_ref=dst, send_sem=send_sems.at[k], recv_sem=recv_sems.at[k],
            device_id=device, device_id_type=MESH,
        )
        c.start()
        copies.append(c)
        return c

    def wait_all(cs):
        for c in cs:
            c.wait_recv()

    stores = []

    def keep(src, dst):
        c = pltpu.make_async_copy(src, dst, local_sems.at[7 + len(stores)])
        c.start()
        stores.append(c)

    barrier = pltpu.get_barrier_semaphore()
    partners = [z_peer] + [at_x(j) for j in range(1, NX)] + [at_y(j) for j in range(1, NY)]
    partners += [at_group(j) for j in range(1, 8)]
    for p in partners:
        pl.semaphore_signal(barrier, inc=1, device_id=p, device_id_type=MESH)
    pairs = (
        (ids_hbm, ids_ref), (gates_hbm, gates_ref), (tok_hbm, tok_ref), (cot_hbm, cot_ref),
        (wg_hbm, wg_ref.at[0]), (wu_hbm, wu_ref.at[0]), (wd_hbm, wd_ref.at[0]),
    )
    loads = []
    for i, (src, dst) in enumerate(pairs):
        c = pltpu.make_async_copy(src, dst, local_sems.at[i])
        c.start()
        loads.append(c)
    for c in loads[:4]:
        c.wait()

    chosen = (ids_ref[...] == 0).astype(F32)
    gate_row = jnp.sum(chosen * gates_ref[...], axis=0, keepdims=True)
    picked = jnp.broadcast_to(jnp.max(chosen, axis=0, keepdims=True), (BLK, TOK))
    ri = lax.broadcasted_iota(jnp.int32, (TOK, TOK), 0)
    ci = lax.broadcasted_iota(jnp.int32, (TOK, TOK), 1)
    eye = (ci == ri).astype(F32)
    before = dot_nn(picked.astype(BF16), (ri < ci).astype(F32).astype(BF16))
    slot = lax.broadcasted_iota(jnp.int32, (BLK, TOK), 0)
    hit = jnp.where((before == slot.astype(F32)) & (slot < CAP), picked, 0.0)
    sel = hit.astype(BF16)
    slot_gate = jnp.sum(hit * gate_row, axis=1, keepdims=True)
    g4[0] = dot_nn(sel, tok_ref[...]).astype(BF16)
    g8[0] = (slot_gate * dot_nn(sel, cot_ref[...])).astype(BF16)

    perm_ref[...] = order_table()
    pl.semaphore_wait(barrier, len(partners))

    def y_start(buf):
        two = [send(buf.at[0], buf.at[j], at_y(j)) for j in (2, 6)]
        return two, [send(buf.at[0], buf.at[j], at_y(j)) for j in (1, 7)]

    def y_relay(buf, cut, started):
        two, rest = started
        n = buf.shape[1]
        lo, hi = pl.ds(0, cut), pl.ds(cut, n - cut)
        two[0].wait_recv()
        rest.append(send(buf.at[2, lo], buf.at[4, lo], at_y(2)))
        rest.append(send(buf.at[2], buf.at[3], at_y(1)))
        two[1].wait_recv()
        rest.append(send(buf.at[6, hi], buf.at[4, hi], at_y(6)))
        rest.append(send(buf.at[6], buf.at[5], at_y(7)))
        return rest

    x_lo, x_hi = pl.ds(0, RA // 2), pl.ds(RA // 2, RA // 2)

    def x_start(buf):
        first = [send(buf.at[0, x_lo], buf.at[1, x_lo], at_x(1)), send(buf.at[0, x_hi], buf.at[3, x_hi], at_x(3))]
        return first, [
            send(buf.at[0, x_hi], buf.at[1, x_hi], at_x(1)), send(buf.at[0, x_lo], buf.at[3, x_lo], at_x(3))
        ]

    def x_relay(buf, started):
        first, rest = started
        first[0].wait_recv()
        rest.append(send(buf.at[1, x_lo], buf.at[2, x_lo], at_x(1)))
        first[1].wait_recv()
        rest.append(send(buf.at[3, x_hi], buf.at[2, x_hi], at_x(3)))
        return rest

    def pack(table, blocks):
        n, _, _ = blocks.shape
        return dot_nn(table[...], blocks.reshape(n * BLK, WID)).astype(BF16)

    far_first_x = (2, 1, 3)
    cx = [send(g4.at[0], g4.at[j], at_x(j)) for j in far_first_x]
    ys = y_start(g8)
    for c in loads[4:]:
        c.wait()
    cz = [send(w.at[0], w.at[1], z_peer) for w in (wg_ref, wu_ref, wd_ref)]
    tb_ref[...] = pack_table(NX)
    ta_ref[...] = pack_table(NY)
    wait_all(cx)
    big8[0] = pack(tb_ref, g4[...])
    y_big = y_start(big8)
    ys = y_relay(g8, BLK // 2, ys)
    wait_all(ys)
    big4[0] = pack(ta_ref, g8[...])
    x_big = x_start(big4)
    y_big = y_relay(big8, RB_CUT, y_big)
    x_big = x_relay(big4, x_big)
    wait_all(cz)

    def partials(ch, arr, rows):
        if arr == 0:
            part[ch, 0] = dot_nt(rows, wg_ref[ch]).astype(BF16).reshape(8, OWN, HID)
            part[ch, 1] = dot_nt(rows, wu_ref[ch]).astype(BF16).reshape(8, OWN, HID)
        else:
            part[ch, 2] = dot_nt(rows, wd_ref[ch]).astype(BF16).reshape(8, OWN, HID)
        ks = pl.ds(0, 2) if arr == 0 else pl.ds(2, 1)
        return send(part.at[ch, ks, pl.ds((1 - core) * NZL, NZL)], core_in.at[ch, ks], core_peer)

    def core_reduce(ch, arr, c):
        c.wait_recv()
        ks = pl.ds(0, 2) if arr == 0 else pl.ds(2, 1)
        mine = part[ch, ks, pl.ds(core * NZL, NZL)]
        core_sum[ch, ks] = (mine.astype(F32) + core_in[ch, ks].astype(F32)).astype(BF16)
        return [
            send(core_sum.at[ch, ks, lax.rem(zl + j, NZL)], z_in.at[ch, ks, j - 1], at_zl(j))
            for j in (3, 1, 2)
        ]

    def totals(ch, k):
        tot = core_sum[ch, k, zl].astype(F32)
        for j in range(3):
            tot = tot + z_in[ch, k, j].astype(F32)
        return tot

    own_row = core * NZL + zl

    def share(ch, ks):
        mine = acts.at[ch, ks, own_row]
        cs = {j: send(mine, mine, at_zl(j)) for j in (3, 1, 2)}
        return cs, [send(mine, mine, core_peer)], ks

    def act_forward(ch, cs):
        wait_all(cs)
        gate_act, up_act = totals(ch, 0), totals(ch, 1)
        sig = jax.nn.sigmoid(gate_act)
        silu = gate_act * sig
        acts[ch, 0, own_row] = (silu * up_act).astype(BF16)
        return share(ch, pl.ds(0, 1)), (silu, up_act * (sig * (1.0 + gate_act * (1.0 - sig))))

    def act_backward(ch, cs, kept):
        wait_all(cs)
        hidden_grad = totals(ch, 2)
        acts[ch, 1, own_row] = (hidden_grad * kept[1]).astype(BF16)
        acts[ch, 2, own_row] = (hidden_grad * kept[0]).astype(BF16)
        return share(ch, pl.ds(1, 2))

    def to_core(ch, shared):
        cs, near, ks = shared
        for j in (1, 3, 2):
            cs[j].wait_recv()
            theirs = acts.at[ch, ks, core * NZL + lax.rem(zl + NZL - j, NZL)]
            near.append(send(theirs, theirs, core_peer))
        return near

    def tok_rows():
        return big8[...].reshape(HALF, WID)

    wait_all(y_big)
    core_t = [partials(h, 0, tok_rows()) for h in range(2)]
    zt = [core_reduce(h, 0, core_t[h]) for h in range(2)]
    wait_all(x_big)
    ordered[...] = dot_nn(perm_ref[...], big4[...].reshape(HALF, WID)).astype(BF16)
    core_g = [partials(h, 1, ordered[...]) for h in range(2)]
    zg = [core_reduce(h, 1, core_g[h]) for h in range(2)]
    f0, kept_0 = act_forward(0, zt[0])
    f1, kept_1 = act_forward(1, zt[1])
    b0 = act_backward(0, zg[0], kept_0)
    b1 = act_backward(1, zg[1], kept_1)

    def product(k, w_ref):
        return dot_nn(acts[0, k].reshape(HALF, HID), w_ref[0]) + dot_nn(acts[1, k].reshape(HALF, HID), w_ref[1])

    def add(*parts):
        tot = parts[0].astype(F32)
        for p in parts[1:]:
            tot = tot + p.astype(F32)
        return tot

    def x_back_start():
        far = [
            send(e4.at[2, x_lo], x_far.at[x_lo], at_x(1)), send(e4.at[2, x_hi], x_far.at[x_hi], at_x(3))
        ]
        return far, [
            send(e4.at[3, x_hi], x_in.at[1, x_hi], at_x(1)), send(e4.at[1, x_lo], x_in.at[0, x_lo], at_x(3))
        ]

    def x_back_relay(started):
        far, rest = started
        far[0].wait_recv()
        e4[3, x_lo] = add(e4[3, x_lo], x_far[x_lo]).astype(BF16)
        rest.append(send(e4.at[3, x_lo], x_in.at[1, x_lo], at_x(1)))
        far[1].wait_recv()
        e4[1, x_hi] = add(e4[1, x_hi], x_far[x_hi]).astype(BF16)
        rest.append(send(e4.at[1, x_hi], x_in.at[0, x_hi], at_x(3)))
        return rest

    def y_back_start(buf, far, half, inn, cut):
        n = buf.shape[1]
        lo, hi = pl.ds(0, cut), pl.ds(cut, n - cut)
        first = [
            send(buf.at[4, lo], half.at[lo], at_y(6)), send(buf.at[3], far.at[0], at_y(7)),
            send(buf.at[4, hi], half.at[hi], at_y(2)), send(buf.at[5], far.at[1], at_y(1)),
        ]
        return first, [send(buf.at[1], inn.at[0], at_y(7)), send(buf.at[7], inn.at[1], at_y(1))]

    def y_back_relay(buf, far, half, inn, cut, started):
        n = buf.shape[1]
        lo, hi = pl.ds(0, cut), pl.ds(cut, n - cut)
        first, rest = started
        wait_all(first[:2])
        buf[2, lo] = add(buf[2, lo], far[0, lo], half[lo]).astype(BF16)
        buf[2, hi] = add(buf[2, hi], far[0, hi]).astype(BF16)
        rest.append(send(buf.at[2], inn.at[2], at_y(6)))
        wait_all(first[2:])
        buf[6, lo] = add(buf[6, lo], far[1, lo]).astype(BF16)
        buf[6, hi] = add(buf[6, hi], far[1, hi], half[hi]).astype(BF16)
        rest.append(send(buf.at[6], inn.at[3], at_y(2)))
        return rest

    def y_total(buf, inn):
        return add(buf[0], inn[0], inn[1], inn[2], inn[3])

    def unpack(table, tot):
        return dot_tn(table[...], tot.astype(BF16)).astype(BF16)

    small_back = (u8, y_far8, y_half8, y_in8, BLK // 2)
    big_back = (e8, y_far_big, y_half_big, y_in_big, RB_CUT)

    def weight_grad(h, k, rows):
        return dot_tn(acts[h, k].reshape(HALF, HID), rows)

    def grad_rows(k):
        return ordered[...] if k == 0 else tok_rows()

    near0, near1 = to_core(0, f0), to_core(1, f1)
    wait_all(near0 + near1)
    e8[...] = product(0, wd_ref).astype(BF16).reshape(NY, RB, WID)
    y_big = y_back_start(*big_back)
    near0, near1 = to_core(0, b0), to_core(1, b1)
    wait_all(near0 + near1)
    e4[...] = dot_tn(perm_ref[...], (product(1, wg_ref) + product(2, wu_ref)).astype(BF16)).astype(BF16).reshape(
        NX, RA, WID
    )
    x_big = x_back_start()
    cz = {}

    def swap_grad(k):
        dw_out[k] = weight_grad(1, k, grad_rows(k)).astype(BF16)
        cz[k] = send(dw_out.at[k], dw_in.at[k], z_peer)

    y_big = y_back_relay(*big_back, y_big)
    for k in (1, 2, 0):
        swap_grad(k)
    x_big = x_back_relay(x_big)
    outs = {1: (dwg_ref, dwg_hbm), 2: (dwu_ref, dwu_hbm), 0: (dwd_ref, dwd_hbm)}
    outs[1][0][...] = weight_grad(0, 1, grad_rows(1))
    wait_all(y_big)
    u4[...] = unpack(tb_ref, y_total(e8, y_in_big)).reshape(NX, BLK, WID)
    cx = [send(u4.at[k], u4_in.at[k - 1], at_x(NX - k)) for k in far_first_x]
    wait_all(x_big)
    u8[...] = unpack(ta_ref, add(e4[0], x_in[0], x_in[1])).reshape(NY, BLK, WID)
    ys = y_back_start(*small_back)
    outs[2][0][...] = weight_grad(0, 2, grad_rows(2))
    wait_all(cx)
    out_rows = dot_tn(sel, add(u4[0], u4_in[0], u4_in[1], u4_in[2]).astype(BF16))
    gate_term = jnp.sum(cot_ref[...].astype(F32) * out_rows, axis=1, keepdims=True)
    row = jnp.sum(gate_term * eye, axis=0, keepdims=True)
    gsum[g] = jnp.broadcast_to(row, (8, TOK))
    cg = [send(gsum.at[g], gsum.at[g], at_group(j)) for j in (4, 3, 5, 2, 6, 1, 7)]
    ys = y_back_relay(*small_back, ys)
    outs[0][0][...] = weight_grad(0, 0, grad_rows(0))
    token_gate = jnp.sum(eye * gate_row, axis=1, keepdims=True)
    mixed_ref[...] = (token_gate * out_rows).astype(BF16)
    keep(mixed_ref, mixed_hbm)
    for k in (1, 2, 0):
        cz[k].wait_recv()
        outs[k][0][...] += dw_in[k].astype(F32)
        keep(*outs[k])
    wait_all(ys)
    tgrad_ref[...] = dot_tn(sel, y_total(u8, y_in8).astype(BF16)).astype(BF16)
    keep(tgrad_ref, tgrad_hbm)
    wait_all(cg)
    tot = gsum[0]
    for j in range(1, 8):
        tot = tot + gsum[j]
    ggrad_ref[...] = chosen * tot[0:1]
    keep(ggrad_ref, ggrad_hbm)
    for c in copies:
        c.wait_send()
    for c in stores:
        c.wait()


def store(*refs):
    ins, outs, mids, in_sems, out_sems = refs[:6], refs[6:12], refs[12:18], refs[18], refs[19]
    loads = [pltpu.make_async_copy(a, m, in_sems.at[i]) for i, (a, m) in enumerate(zip(ins, mids))]
    saves = [pltpu.make_async_copy(m, b, out_sems.at[i]) for i, (m, b) in enumerate(zip(mids, outs))]
    for c in loads:
        c.start()
    for load, save in zip(loads, saves):
        load.wait()
        save.start()
    for c in saves:
        c.wait()


def on_device(tokens, expert_ids, gates, gate_weight, up_weight, down_weight, cotangent):
    def vm(*shape, kind=BF16):
        return pltpu.VMEM(shape, kind)

    scratch = [
        vm(TOK, WID), vm(TOK, WID), vm(2, TOK, kind=F32),
        vm(HID, WID, kind=F32), vm(HID, WID, kind=F32), vm(HID, WID, kind=F32),
        vm(2, TOK, kind=jnp.int32), vm(2, TOK, kind=F32), vm(TOK, WID), vm(TOK, WID),
        vm(2, HID, WID), vm(2, HID, WID), vm(2, HID, WID),
        vm(NY, BLK, WID), vm(NX, BLK, WID), vm(NX, RA, WID), vm(NY, RB, WID), vm(HALF, WID),
        vm(2, 3, 8, OWN, HID), vm(2, 3, NZL, OWN, HID), vm(2, 3, NZL, OWN, HID),
        vm(2, 3, 3, OWN, HID), vm(2, 3, 8, OWN, HID),
        vm(NX, RA, WID), vm(2, RA, WID), vm(RA, WID),
        vm(NY, RB, WID), vm(4, RB, WID), vm(2, RB, WID), vm(RB, WID),
        vm(NY, BLK, WID), vm(4, BLK, WID), vm(2, BLK, WID), vm(BLK, WID),
        vm(NX, BLK, WID), vm(NX - 1, BLK, WID),
        vm(3, HID, WID), vm(3, HID, WID), vm(8, 8, TOK, kind=F32),
        vm(RA, NY * BLK), vm(RB, NX * BLK), vm(HALF, HALF),
        pltpu.SemaphoreType.DMA((13,)),
        pltpu.SemaphoreType.DMA((N_COPIES,)), pltpu.SemaphoreType.DMA((N_COPIES,)),
    ]
    half = jax.ShapeDtypeStruct((TOK, WID), BF16)
    full = jax.ShapeDtypeStruct((TOK, WID), F32)
    shapes = (half, half, jax.ShapeDtypeStruct((2, TOK), F32), full, full, full)
    results = pl.pallas_call(
        kernel,
        out_shape=shapes,
        in_specs=[pl.BlockSpec(memory_space=pl.ANY)] * 7,
        out_specs=[pl.BlockSpec(memory_space=pl.ANY)] * 6,
        scratch_shapes=scratch,
        compiler_params=pltpu.CompilerParams(
            collective_id=0, has_side_effects=True, vmem_limit_bytes=VMEM_BYTES
        ),
    )(expert_ids.T, gates.T, tokens, cotangent, gate_weight, up_weight, down_weight)
    mixed, tgrad, ggrad, dwg, dwu, dwd = pl.pallas_call(
        store,
        out_shape=shapes,
        in_specs=[pl.BlockSpec(memory_space=pl.ANY)] * 6,
        out_specs=[pl.BlockSpec(memory_space=pl.ANY)] * 6,
        scratch_shapes=scratch[:6] + [pltpu.SemaphoreType.DMA((6,))] * 2,
        compiler_params=pltpu.CompilerParams(vmem_limit_bytes=VMEM_BYTES),
    )(*results)
    return mixed, tgrad, ggrad.T, dwg, dwu, dwd


def solution(mesh):
    wide, narrow = P("dp", "group"), P("dp", None)
    return jax.shard_map(
        on_device,
        mesh=mesh,
        in_specs=(wide, narrow, narrow, wide, wide, wide, wide),
        out_specs=(wide, wide, narrow, wide, wide, wide),
        check_vma=False,
    )
```

```python
import jax
import jax.numpy as jnp
from jax import lax
from jax.experimental import pallas as pl
from jax.experimental.pallas import tpu as pltpu
from jax.sharding import PartitionSpec as P

MESH = pl.DeviceIdType.MESH
F32 = jnp.float32
BF16 = jnp.bfloat16
CAP = 20
BLK = 32
NX, NY, NZL = 4, 8, 4
TOK, WID, HID = 128, 384, 128
RA = NY * CAP
RB = NX * CAP
HALF = NX * NY * CAP
OWN = HALF // 8
RB_CUT = 48
N_COPIES = 192
VMEM_BYTES = 64 * 1024 * 1024 - 64 * 1024


def dot_nt(a, b):
    return lax.dot_general(a, b, (((1,), (1,)), ((), ())), preferred_element_type=F32)


def dot_tn(a, b):
    return lax.dot_general(a, b, (((0,), (0,)), ((), ())), preferred_element_type=F32)


def dot_nn(a, b):
    return jnp.dot(a, b, preferred_element_type=F32)


def pack_table(blocks):
    rows, cols = blocks * CAP, blocks * BLK
    r = lax.broadcasted_iota(jnp.int32, (rows, cols), 0)
    c = lax.broadcasted_iota(jnp.int32, (rows, cols), 1)
    src = r
    for k in range(1, blocks):
        src = src + jnp.where(r >= k * CAP, BLK - CAP, 0)
    return (src == c).astype(F32).astype(BF16)


def order_table():
    r = lax.broadcasted_iota(jnp.int32, (HALF, TOK), 0)
    y = jnp.zeros_like(r)
    for k in range(1, NY):
        y = y + (r >= k * RB).astype(jnp.int32)
    x, q = jnp.zeros_like(r), r - y * RB
    for k in range(1, NX):
        x = x + (q >= k * CAP).astype(jnp.int32)
    src = x * RA + y * CAP + q - x * CAP
    c = lax.broadcasted_iota(jnp.int32, (HALF, TOK), 1)
    return jnp.concatenate(
        [(src == c + k * TOK).astype(F32).astype(BF16) for k in range(HALF // TOK)], axis=1
    )


def kernel(
    ids_hbm, gates_hbm, tok_hbm, cot_hbm, wg_hbm, wu_hbm, wd_hbm,
    mixed_hbm, tgrad_hbm, ggrad_hbm, dwg_hbm, dwu_hbm, dwd_hbm,
    mixed_ref, tgrad_ref, ggrad_ref, dwg_ref, dwu_ref, dwd_ref,
    ids_ref, gates_ref, tok_ref, cot_ref, wg_ref, wu_ref, wd_ref,
    g8, g4, big4, big8, ordered, part, core_in, core_sum, z_in, acts,
    e4, x_in, x_far, e8, y_in_big, y_far_big, y_half_big, u8, y_in8, y_far8, y_half8, u4, u4_in,
    dw_out, dw_in, gsum, ta_ref, tb_ref, perm_ref,
    local_sems, send_sems, recv_sems,
):
    d = lax.axis_index("dp")
    g = lax.axis_index("group")
    x = lax.rem(d, NX)
    y = lax.rem(lax.div(d, NX), NY)
    z = lax.div(d, NX * NY)
    core = lax.rem(g, 2)
    zl = lax.div(g, 2)

    def at_x(j):
        return {"dp": z * (NX * NY) + y * NX + lax.rem(x + j, NX)}

    def at_y(j):
        return {"dp": z * (NX * NY) + lax.rem(y + j, NY) * NX + x}

    z_peer = {"dp": (1 - z) * (NX * NY) + y * NX + x}
    core_peer = {"group": zl * 2 + (1 - core)}

    def at_zl(j):
        return {"group": lax.rem(zl + j, NZL) * 2 + core}

    def at_group(j):
        return {"group": lax.rem(g + j, 8)}

    copies = []

    def send(src, dst, device):
        k = len(copies)
        c = pltpu.make_async_remote_copy(
            src_ref=src, dst_ref=dst, send_sem=send_sems.at[k], recv_sem=recv_sems.at[k],
            device_id=device, device_id_type=MESH,
        )
        c.start()
        copies.append(c)
        return c

    def wait_all(cs):
        for c in cs:
            c.wait_recv()

    stores = []

    def keep(src, dst):
        c = pltpu.make_async_copy(src, dst, local_sems.at[7 + len(stores)])
        c.start()
        stores.append(c)

    barrier = pltpu.get_barrier_semaphore()
    partners = [z_peer] + [at_x(j) for j in range(1, NX)] + [at_y(j) for j in range(1, NY)]
    partners += [at_group(j) for j in range(1, 8)]
    for p in partners:
        pl.semaphore_signal(barrier, inc=1, device_id=p, device_id_type=MESH)
    pairs = (
        (ids_hbm, ids_ref), (gates_hbm, gates_ref), (tok_hbm, tok_ref), (cot_hbm, cot_ref),
        (wg_hbm, wg_ref.at[0]), (wu_hbm, wu_ref.at[0]), (wd_hbm, wd_ref.at[0]),
    )
    loads = []
    for i, (src, dst) in enumerate(pairs):
        c = pltpu.make_async_copy(src, dst, local_sems.at[i])
        c.start()
        loads.append(c)
    for c in loads[:4]:
        c.wait()

    chosen = (ids_ref[...] == 0).astype(F32)
    gate_row = jnp.sum(chosen * gates_ref[...], axis=0, keepdims=True)
    picked = jnp.broadcast_to(jnp.max(chosen, axis=0, keepdims=True), (BLK, TOK))
    ri = lax.broadcasted_iota(jnp.int32, (TOK, TOK), 0)
    ci = lax.broadcasted_iota(jnp.int32, (TOK, TOK), 1)
    eye = (ci == ri).astype(F32)
    before = dot_nn(picked.astype(BF16), (ri < ci).astype(F32).astype(BF16))
    slot = lax.broadcasted_iota(jnp.int32, (BLK, TOK), 0)
    hit = jnp.where((before == slot.astype(F32)) & (slot < CAP), picked, 0.0)
    sel = hit.astype(BF16)
    slot_gate = jnp.sum(hit * gate_row, axis=1, keepdims=True)
    g4[0] = dot_nn(sel, tok_ref[...]).astype(BF16)
    g8[0] = (slot_gate * dot_nn(sel, cot_ref[...])).astype(BF16)

    pl.semaphore_wait(barrier, len(partners))

    def y_start(buf):
        two = [send(buf.at[0], buf.at[j], at_y(j)) for j in (2, 6)]
        return two, [send(buf.at[0], buf.at[j], at_y(j)) for j in (1, 7)]

    def y_relay(buf, cut, started):
        two, rest = started
        n = buf.shape[1]
        lo, hi = pl.ds(0, cut), pl.ds(cut, n - cut)
        two[0].wait_recv()
        rest.append(send(buf.at[2, lo], buf.at[4, lo], at_y(2)))
        rest.append(send(buf.at[2], buf.at[3], at_y(1)))
        two[1].wait_recv()
        rest.append(send(buf.at[6, hi], buf.at[4, hi], at_y(6)))
        rest.append(send(buf.at[6], buf.at[5], at_y(7)))
        return rest

    x_lo, x_hi = pl.ds(0, RA // 2), pl.ds(RA // 2, RA // 2)

    def x_start(buf):
        first = [send(buf.at[0, x_lo], buf.at[1, x_lo], at_x(1)), send(buf.at[0, x_hi], buf.at[3, x_hi], at_x(3))]
        return first, [
            send(buf.at[0, x_hi], buf.at[1, x_hi], at_x(1)), send(buf.at[0, x_lo], buf.at[3, x_lo], at_x(3))
        ]

    def x_relay(buf, started):
        first, rest = started
        first[0].wait_recv()
        rest.append(send(buf.at[1, x_lo], buf.at[2, x_lo], at_x(1)))
        first[1].wait_recv()
        rest.append(send(buf.at[3, x_hi], buf.at[2, x_hi], at_x(3)))
        return rest

    def pack(table, blocks):
        n, _, _ = blocks.shape
        return dot_nn(table[...], blocks.reshape(n * BLK, WID)).astype(BF16)

    far_first_x = (2, 1, 3)
    cx = [send(g4.at[0], g4.at[j], at_x(j)) for j in far_first_x]
    ys = y_start(g8)
    for c in loads[4:]:
        c.wait()
    cz = [send(w.at[0], w.at[1], z_peer) for w in (wg_ref, wu_ref, wd_ref)]
    tb_ref[...] = pack_table(NX)
    ta_ref[...] = pack_table(NY)
    perm_ref[...] = order_table()
    wait_all(cx)
    big8[0] = pack(tb_ref, g4[...])
    y_big = y_start(big8)
    ys = y_relay(g8, BLK // 2, ys)
    wait_all(ys)
    big4[0] = pack(ta_ref, g8[...])
    x_big = x_start(big4)
    y_big = y_relay(big8, RB_CUT, y_big)
    x_big = x_relay(big4, x_big)
    wait_all(cz)

    def partials(ch, arr, rows):
        if arr == 0:
            part[ch, 0] = dot_nt(rows, wg_ref[ch]).astype(BF16).reshape(8, OWN, HID)
            part[ch, 1] = dot_nt(rows, wu_ref[ch]).astype(BF16).reshape(8, OWN, HID)
        else:
            part[ch, 2] = dot_nt(rows, wd_ref[ch]).astype(BF16).reshape(8, OWN, HID)
        ks = pl.ds(0, 2) if arr == 0 else pl.ds(2, 1)
        return send(part.at[ch, ks, pl.ds((1 - core) * NZL, NZL)], core_in.at[ch, ks], core_peer)

    def core_reduce(ch, arr, c):
        c.wait_recv()
        ks = pl.ds(0, 2) if arr == 0 else pl.ds(2, 1)
        mine = part[ch, ks, pl.ds(core * NZL, NZL)]
        core_sum[ch, ks] = (mine.astype(F32) + core_in[ch, ks].astype(F32)).astype(BF16)
        return [
            send(core_sum.at[ch, ks, lax.rem(zl + j, NZL)], z_in.at[ch, ks, j - 1], at_zl(j))
            for j in (3, 1, 2)
        ]

    def totals(ch, k):
        tot = core_sum[ch, k, zl].astype(F32)
        for j in range(3):
            tot = tot + z_in[ch, k, j].astype(F32)
        return tot

    own_row = core * NZL + zl

    def share(ch, ks):
        mine = acts.at[ch, ks, own_row]
        cs = {j: send(mine, mine, at_zl(j)) for j in (3, 1, 2)}
        return cs, [send(mine, mine, core_peer)], ks

    def act_forward(ch, cs):
        wait_all(cs)
        gate_act, up_act = totals(ch, 0), totals(ch, 1)
        sig = jax.nn.sigmoid(gate_act)
        silu = gate_act * sig
        acts[ch, 0, own_row] = (silu * up_act).astype(BF16)
        return share(ch, pl.ds(0, 1)), (silu, up_act * (sig * (1.0 + gate_act * (1.0 - sig))))

    def act_backward(ch, cs, kept):
        wait_all(cs)
        hidden_grad = totals(ch, 2)
        acts[ch, 1, own_row] = (hidden_grad * kept[1]).astype(BF16)
        acts[ch, 2, own_row] = (hidden_grad * kept[0]).astype(BF16)
        return share(ch, pl.ds(1, 2))

    def to_core(ch, shared):
        cs, near, ks = shared
        for j in (1, 3, 2):
            cs[j].wait_recv()
            theirs = acts.at[ch, ks, core * NZL + lax.rem(zl + NZL - j, NZL)]
            near.append(send(theirs, theirs, core_peer))
        return near

    def tok_rows():
        return big8[...].reshape(HALF, WID)

    wait_all(y_big)
    core_t = [partials(h, 0, tok_rows()) for h in range(2)]
    zt = [core_reduce(h, 0, core_t[h]) for h in range(2)]
    wait_all(x_big)
    ordered[...] = dot_nn(perm_ref[...], big4[...].reshape(HALF, WID)).astype(BF16)
    core_g = [partials(h, 1, ordered[...]) for h in range(2)]
    zg = [core_reduce(h, 1, core_g[h]) for h in range(2)]
    f0, kept_0 = act_forward(0, zt[0])
    f1, kept_1 = act_forward(1, zt[1])
    b0 = act_backward(0, zg[0], kept_0)
    b1 = act_backward(1, zg[1], kept_1)

    def product(k, w_ref):
        return dot_nn(acts[0, k].reshape(HALF, HID), w_ref[0]) + dot_nn(acts[1, k].reshape(HALF, HID), w_ref[1])

    def add(*parts):
        tot = parts[0].astype(F32)
        for p in parts[1:]:
            tot = tot + p.astype(F32)
        return tot

    def x_back_start():
        far = [
            send(e4.at[2, x_lo], x_far.at[x_lo], at_x(1)), send(e4.at[2, x_hi], x_far.at[x_hi], at_x(3))
        ]
        return far, [
            send(e4.at[3, x_hi], x_in.at[1, x_hi], at_x(1)), send(e4.at[1, x_lo], x_in.at[0, x_lo], at_x(3))
        ]

    def x_back_relay(started):
        far, rest = started
        far[0].wait_recv()
        e4[3, x_lo] = add(e4[3, x_lo], x_far[x_lo]).astype(BF16)
        rest.append(send(e4.at[3, x_lo], x_in.at[1, x_lo], at_x(1)))
        far[1].wait_recv()
        e4[1, x_hi] = add(e4[1, x_hi], x_far[x_hi]).astype(BF16)
        rest.append(send(e4.at[1, x_hi], x_in.at[0, x_hi], at_x(3)))
        return rest

    def y_back_start(buf, far, half, inn, cut):
        n = buf.shape[1]
        lo, hi = pl.ds(0, cut), pl.ds(cut, n - cut)
        first = [
            send(buf.at[4, lo], half.at[lo], at_y(6)), send(buf.at[3], far.at[0], at_y(7)),
            send(buf.at[4, hi], half.at[hi], at_y(2)), send(buf.at[5], far.at[1], at_y(1)),
        ]
        return first, [send(buf.at[1], inn.at[0], at_y(7)), send(buf.at[7], inn.at[1], at_y(1))]

    def y_back_relay(buf, far, half, inn, cut, started):
        n = buf.shape[1]
        lo, hi = pl.ds(0, cut), pl.ds(cut, n - cut)
        first, rest = started
        wait_all(first[:2])
        buf[2, lo] = add(buf[2, lo], far[0, lo], half[lo]).astype(BF16)
        buf[2, hi] = add(buf[2, hi], far[0, hi]).astype(BF16)
        rest.append(send(buf.at[2], inn.at[2], at_y(6)))
        wait_all(first[2:])
        buf[6, lo] = add(buf[6, lo], far[1, lo]).astype(BF16)
        buf[6, hi] = add(buf[6, hi], far[1, hi], half[hi]).astype(BF16)
        rest.append(send(buf.at[6], inn.at[3], at_y(2)))
        return rest

    def y_total(buf, inn):
        return add(buf[0], inn[0], inn[1], inn[2], inn[3])

    def unpack(table, tot):
        return dot_tn(table[...], tot.astype(BF16)).astype(BF16)

    small_back = (u8, y_far8, y_half8, y_in8, BLK // 2)
    big_back = (e8, y_far_big, y_half_big, y_in_big, RB_CUT)

    def weight_grad(h, k, rows):
        return dot_tn(acts[h, k].reshape(HALF, HID), rows)

    def grad_rows(k):
        return ordered[...] if k == 0 else tok_rows()

    near0, near1 = to_core(0, f0), to_core(1, f1)
    wait_all(near0 + near1)
    e8[...] = product(0, wd_ref).astype(BF16).reshape(NY, RB, WID)
    y_big = y_back_start(*big_back)
    near0, near1 = to_core(0, b0), to_core(1, b1)
    wait_all(near0 + near1)
    e4[...] = dot_tn(perm_ref[...], (product(1, wg_ref) + product(2, wu_ref)).astype(BF16)).astype(BF16).reshape(
        NX, RA, WID
    )
    x_big = x_back_start()
    cz = {}

    def swap_grad(k):
        dw_out[k] = weight_grad(1, k, grad_rows(k)).astype(BF16)
        cz[k] = send(dw_out.at[k], dw_in.at[k], z_peer)

    y_big = y_back_relay(*big_back, y_big)
    for k in (1, 2, 0):
        swap_grad(k)
    x_big = x_back_relay(x_big)
    outs = {1: (dwg_ref, dwg_hbm), 2: (dwu_ref, dwu_hbm), 0: (dwd_ref, dwd_hbm)}
    outs[1][0][...] = weight_grad(0, 1, grad_rows(1))
    wait_all(y_big)
    u4[...] = unpack(tb_ref, y_total(e8, y_in_big)).reshape(NX, BLK, WID)
    cx = [send(u4.at[k], u4_in.at[k - 1], at_x(NX - k)) for k in far_first_x]
    wait_all(x_big)
    u8[...] = unpack(ta_ref, add(e4[0], x_in[0], x_in[1])).reshape(NY, BLK, WID)
    ys = y_back_start(*small_back)
    outs[2][0][...] = weight_grad(0, 2, grad_rows(2))
    wait_all(cx)
    out_rows = dot_tn(sel, add(u4[0], u4_in[0], u4_in[1], u4_in[2]).astype(BF16))
    gate_term = jnp.sum(cot_ref[...].astype(F32) * out_rows, axis=1, keepdims=True)
    row = jnp.sum(gate_term * eye, axis=0, keepdims=True)
    gsum[g] = jnp.broadcast_to(row, (8, TOK))
    cg = [send(gsum.at[g], gsum.at[g], at_group(j)) for j in (4, 3, 5, 2, 6, 1, 7)]
    ys = y_back_relay(*small_back, ys)
    outs[0][0][...] = weight_grad(0, 0, grad_rows(0))
    token_gate = jnp.sum(eye * gate_row, axis=1, keepdims=True)
    mixed_ref[...] = (token_gate * out_rows).astype(BF16)
    keep(mixed_ref, mixed_hbm)
    for k in (1, 2, 0):
        cz[k].wait_recv()
        outs[k][0][...] += dw_in[k].astype(F32)
        keep(*outs[k])
    wait_all(ys)
    tgrad_ref[...] = dot_tn(sel, y_total(u8, y_in8).astype(BF16)).astype(BF16)
    keep(tgrad_ref, tgrad_hbm)
    wait_all(cg)
    tot = gsum[0]
    for j in range(1, 8):
        tot = tot + gsum[j]
    ggrad_ref[...] = chosen * tot[0:1]
    keep(ggrad_ref, ggrad_hbm)
    for c in copies:
        c.wait_send()
    for c in stores:
        c.wait()


def store(*refs):
    ins, outs, mids, in_sems, out_sems = refs[:6], refs[6:12], refs[12:18], refs[18], refs[19]
    loads = [pltpu.make_async_copy(a, m, in_sems.at[i]) for i, (a, m) in enumerate(zip(ins, mids))]
    saves = [pltpu.make_async_copy(m, b, out_sems.at[i]) for i, (m, b) in enumerate(zip(mids, outs))]
    for c in loads:
        c.start()
    for load, save in zip(loads, saves):
        load.wait()
        save.start()
    for c in saves:
        c.wait()


def on_device(tokens, expert_ids, gates, gate_weight, up_weight, down_weight, cotangent):
    def vm(*shape, kind=BF16):
        return pltpu.VMEM(shape, kind)

    scratch = [
        vm(TOK, WID), vm(TOK, WID), vm(2, TOK, kind=F32),
        vm(HID, WID, kind=F32), vm(HID, WID, kind=F32), vm(HID, WID, kind=F32),
        vm(2, TOK, kind=jnp.int32), vm(2, TOK, kind=F32), vm(TOK, WID), vm(TOK, WID),
        vm(2, HID, WID), vm(2, HID, WID), vm(2, HID, WID),
        vm(NY, BLK, WID), vm(NX, BLK, WID), vm(NX, RA, WID), vm(NY, RB, WID), vm(HALF, WID),
        vm(2, 3, 8, OWN, HID), vm(2, 3, NZL, OWN, HID), vm(2, 3, NZL, OWN, HID),
        vm(2, 3, 3, OWN, HID), vm(2, 3, 8, OWN, HID),
        vm(NX, RA, WID), vm(2, RA, WID), vm(RA, WID),
        vm(NY, RB, WID), vm(4, RB, WID), vm(2, RB, WID), vm(RB, WID),
        vm(NY, BLK, WID), vm(4, BLK, WID), vm(2, BLK, WID), vm(BLK, WID),
        vm(NX, BLK, WID), vm(NX - 1, BLK, WID),
        vm(3, HID, WID), vm(3, HID, WID), vm(8, 8, TOK, kind=F32),
        vm(RA, NY * BLK), vm(RB, NX * BLK), vm(HALF, HALF),
        pltpu.SemaphoreType.DMA((13,)),
        pltpu.SemaphoreType.DMA((N_COPIES,)), pltpu.SemaphoreType.DMA((N_COPIES,)),
    ]
    half = jax.ShapeDtypeStruct((TOK, WID), BF16)
    full = jax.ShapeDtypeStruct((TOK, WID), F32)
    shapes = (half, half, jax.ShapeDtypeStruct((2, TOK), F32), full, full, full)
    results = pl.pallas_call(
        kernel,
        out_shape=shapes,
        in_specs=[pl.BlockSpec(memory_space=pl.ANY)] * 7,
        out_specs=[pl.BlockSpec(memory_space=pl.ANY)] * 6,
        scratch_shapes=scratch,
        compiler_params=pltpu.CompilerParams(
            collective_id=0, has_side_effects=True, vmem_limit_bytes=VMEM_BYTES
        ),
    )(expert_ids.T, gates.T, tokens, cotangent, gate_weight, up_weight, down_weight)
    mixed, tgrad, ggrad, dwg, dwu, dwd = pl.pallas_call(
        store,
        out_shape=shapes,
        in_specs=[pl.BlockSpec(memory_space=pl.ANY)] * 6,
        out_specs=[pl.BlockSpec(memory_space=pl.ANY)] * 6,
        scratch_shapes=scratch[:6] + [pltpu.SemaphoreType.DMA((6,))] * 2,
        compiler_params=pltpu.CompilerParams(vmem_limit_bytes=VMEM_BYTES),
    )(*results)
    return mixed, tgrad, ggrad.T, dwg, dwu, dwd


def solution(mesh):
    wide, narrow = P("dp", "group"), P("dp", None)
    return jax.shard_map(
        on_device,
        mesh=mesh,
        in_specs=(wide, narrow, narrow, wide, wide, wide, wide),
        out_specs=(wide, wide, narrow, wide, wide, wide),
        check_vma=False,
    )
```
